128 devices in a mesh: region: 8 (over z_lo, y), sub: 16 (over z_hi, x, core).
Axes of the slice: x: 4, y: 4, z: 4 (z_hi: 2, z_lo: 2; z = z_hi * 2 + z_lo), core: 2. Of those that a mesh axis runs over, the one named last changes fastest.
Arguments:
- node_feats: bfloat16 [131072, 512], P(('region', 'sub')), may hold values from -6 to 6
- gain_in: float32 [512], replicated, may hold values from 0.25 to 1.75
- w_qkv: bfloat16 [512, 1536], replicated, may hold values from -4 to 4
- gain_out: float32 [512], replicated, may hold values from 0.25 to 1.75
- w_out: bfloat16 [512, 512], replicated, may hold values from -0.25 to 0.25
- adjacency: int32 [2048, 7], P(('region', 'sub')), may hold values from 0 to 2047, as said below
- fine_valid: int32 [2048, 7], P(('region', 'sub')), may hold values 0 or 1
- coarse_mask: int32 [2048, 40], P(('region', 'sub')), may hold values 0 or 1
- coarse_src: int32 [2560], P(('region', 'sub')), may hold values from 0 to 131071, as said below
Outputs:
- update: bfloat16 [131072, 512], P(('region', 'sub'))
The draws below stay inside these ranges and needn't reach their ends.
Inputs may be any that keep to these rules, and one draw needn't show every extreme that they name: `adjacency`: entry (b, 0) is b itself. Block b is held by device d = b // 16, devices numbered region * 16 + sub; every entry of row b names a block held by d or by a device one step away along region or along sub. `coarse_src`: entry i names a node held by the device that holds entry i: a node from (i // 20) * 16 * 64 to that plus 16 * 64 - 1.
All inputs are finite; a program needn't handle non-finite values. No bound on the sum of `fine_valid` or of `coarse_mask` on one device may be relied on, other than what follows from the above.
Results may differ from the reference program's by a relative error of at most 0.0083.
Values may be sent and summed in bfloat16 or wider, within the bound.
A program may use at most 128 MiB of HBM per device.

```python
import jax
import jax.numpy as jnp
from jax import lax

D = 512
HEADS = 8
BLOCK = 64
NADJ = 7
BLK_DEV = 16
CN_DEV = 20
NBLK = 2048
NODES = 131072
CNODES = 2560
CBLK = 40
N_REGION = 8
N_SUB = 16


def draw_w_qkv(key, part):
    weight_scale = D ** (-0.5)
    return (jnp.clip(jax.random.normal(key, (D, 3 * D), jnp.float32), -4.0, 4.0) * weight_scale).astype(jnp.bfloat16)


def draw_adjacency(key, part):
    total_blocks = BLK_DEV * N_REGION * N_SUB
    block_ids = jnp.arange(total_blocks, dtype=jnp.int32)
    device_ids = block_ids // BLK_DEV
    region_pos = device_ids // N_SUB
    sub_pos = device_ids % N_SUB
    key_dir = jax.random.fold_in(key, 11)
    key_blk = jax.random.fold_in(key, 12)
    direction = jax.random.randint(key_dir, (total_blocks, NADJ), 0, 5)
    local_blk = jax.random.randint(key_blk, (total_blocks, NADJ), 0, BLK_DEV)
    region_step = jnp.array([0, -1, 1, 0, 0], dtype=jnp.int32)[direction]
    sub_step = jnp.array([0, 0, 0, -1, 1], dtype=jnp.int32)[direction]
    region_next = region_pos[:, None] + region_step
    sub_next = sub_pos[:, None] + sub_step
    inside = (region_next >= 0) & (region_next < N_REGION) & (sub_next >= 0) & (sub_next < N_SUB)
    region_next = jnp.where(inside, region_next, region_pos[:, None])
    sub_next = jnp.where(inside, sub_next, sub_pos[:, None])
    picked = (region_next * N_SUB + sub_next) * BLK_DEV + local_blk
    picked = picked.at[:, 0].set(block_ids)
    return picked.astype(jnp.int32)


def draw_coarse_src(key, part):
    total_coarse = CN_DEV * N_REGION * N_SUB
    node_span = BLK_DEV * BLOCK
    owners = jnp.arange(total_coarse, dtype=jnp.int32) // CN_DEV
    offsets = jax.random.randint(jax.random.fold_in(key, 21), (total_coarse,), 0, node_span)
    offsets = offsets.at[0].set(0).at[total_coarse - 1].set(node_span - 1)
    return (owners * node_span + offsets).astype(jnp.int32)


def place_ends(drawn, stream_key, least, top_value):
    index_at = [jax.random.randint(jax.random.fold_in(stream_key, axis), (), 0, length) for axis, length in enumerate(drawn.shape)]
    main_axis = drawn.shape.index(max(drawn.shape))
    beside = index_at[:main_axis] + [(index_at[main_axis] + 1) % drawn.shape[main_axis]] + index_at[main_axis + 1:]
    return drawn.at[tuple(index_at)].set(least).at[tuple(beside)].set(top_value)


def shard_levels(stream_key, extent, split, low, top_value):
    def one(dim, shards_of):
        draws = jax.random.uniform(jax.random.fold_in(jax.random.fold_in(stream_key, 6), dim), (shards_of,), jnp.float32, low / len(split), top_value / len(split))
        return jnp.repeat(jnp.exp(draws), extent[dim] // shards_of).reshape((-1,) + (1,) * (len(extent) - dim - 1))

    factor_of = one(*split[0])
    for cut in split[1:]:
        factor_of = factor_of * one(*cut)
    return factor_of


def noise(key, dims, deviation, bound, cuts=(), kind=jnp.bfloat16):
    loudness = shard_levels(key, dims, cuts, -0.22, 0.18) if cuts else 1.0
    result = jax.random.normal(key, dims, jnp.float32) * deviation * loudness
    return jnp.minimum(jnp.maximum(result, -bound), bound).astype(kind)


def setup_inputs(seed: int = 0) -> dict:
    arg_keys = jax.random.split(jax.random.key(seed), 10)
    node_feats = noise(arg_keys[0], (NODES, D), 1.0, 6.0, ((0, 128),))
    gain_in = jnp.clip(1.0 + 0.15 * jax.random.normal(arg_keys[1], (D,), jnp.float32), 0.25, 1.75)
    w_qkv = draw_w_qkv(jax.random.fold_in(arg_keys[9], 71), 0)
    gain_out = jnp.clip(1.0 + 0.15 * jax.random.normal(arg_keys[3], (D,), jnp.float32), 0.25, 1.75)
    w_out = noise(arg_keys[4], (D, D), D ** -0.5, 0.25)
    adjacency = draw_adjacency(jax.random.fold_in(arg_keys[9], 71), 0)
    fine_valid = place_ends((jax.random.randint(arg_keys[6], (NBLK, NADJ), 0, 4) < 3).astype(jnp.int32), jax.random.fold_in(arg_keys[6], 1), 0, 1)
    coarse_mask = place_ends((jax.random.randint(arg_keys[7], (NBLK, CBLK), 0, 2) < 1).astype(jnp.int32), jax.random.fold_in(arg_keys[7], 1), 0, 1)
    coarse_src = draw_coarse_src(jax.random.fold_in(arg_keys[9], 71), 0)
    return dict(node_feats=node_feats, gain_in=gain_in, w_qkv=w_qkv, gain_out=gain_out, w_out=w_out, adjacency=adjacency, fine_valid=fine_valid, coarse_mask=coarse_mask, coarse_src=coarse_src)


neg_large = -1e+30

def rms_scale(feats, gain):
    vals = feats.astype(jnp.float32)
    mean_square = lax.optimization_barrier(jnp.mean(vals * vals, axis=-1, keepdims=True))
    return (vals * lax.rsqrt(mean_square + 1e-06) * gain.astype(jnp.float32)).astype(jnp.bfloat16)

def reference(node_feats, gain_in, w_qkv, gain_out, w_out, adjacency, fine_valid, coarse_mask, coarse_src):
    head_width = D // HEADS
    score_scale = head_width ** (-0.5)
    normed = rms_scale(node_feats, gain_in)
    projected = jnp.dot(normed, w_qkv, preferred_element_type=jnp.float32).astype(jnp.bfloat16)
    all_queries = projected[:, :D].reshape(NBLK, BLOCK, HEADS, head_width)
    all_keys = projected[:, D:2 * D].reshape(NBLK, BLOCK, HEADS, head_width)
    all_values = projected[:, 2 * D:].reshape(NBLK, BLOCK, HEADS, head_width)
    coarse_rows = projected[coarse_src.astype(jnp.int32)]
    coarse_keys = coarse_rows[:, D:2 * D].reshape(CNODES, HEADS, head_width).astype(jnp.float32)
    coarse_values = coarse_rows[:, 2 * D:].reshape(CNODES, HEADS, head_width).astype(jnp.float32)
    slot_live = (fine_valid == 1) | (jnp.arange(NADJ)[None, :] == 0)

    def one_block(inputs):
        block_q, neighbours, live_slots, coarse_live = inputs
        block_q = block_q.astype(jnp.float32)
        fine_keys = all_keys[neighbours].reshape(NADJ * BLOCK, HEADS, head_width).astype(jnp.float32)
        fine_values = all_values[neighbours].reshape(NADJ * BLOCK, HEADS, head_width).astype(jnp.float32)
        fine_scores = jnp.einsum('qhd,khd->hqk', block_q, fine_keys) * score_scale
        fine_scores = jnp.where(jnp.repeat(live_slots, BLOCK)[None, None, :], fine_scores, neg_large)
        coarse_scores = jnp.einsum('qhd,khd->hqk', block_q, coarse_keys) * score_scale
        coarse_scores = jnp.where(jnp.repeat(coarse_live == 1, BLOCK)[None, None, :], coarse_scores, neg_large)
        score_peak = jnp.maximum(lax.optimization_barrier(jnp.max(fine_scores, axis=-1)), lax.optimization_barrier(jnp.max(coarse_scores, axis=-1)))[..., None]
        fine_exp = jnp.exp(fine_scores - score_peak)
        coarse_exp = jnp.exp(coarse_scores - score_peak)
        total = lax.optimization_barrier(jnp.sum(fine_exp, axis=-1, keepdims=True)) + lax.optimization_barrier(jnp.sum(coarse_exp, axis=-1, keepdims=True))
        fine_weights = (fine_exp / total).astype(jnp.bfloat16).astype(jnp.float32)
        coarse_weights = (coarse_exp / total).astype(jnp.bfloat16).astype(jnp.float32)
        mixed_out = jnp.einsum('hqk,khd->qhd', fine_weights, fine_values)
        mixed_out = mixed_out + jnp.einsum('hqk,khd->qhd', coarse_weights, coarse_values)
        return mixed_out.reshape(BLOCK, D).astype(jnp.bfloat16)
    attended = lax.map(one_block, (all_queries, adjacency.astype(jnp.int32), slot_live, coarse_mask))
    renormed = rms_scale(attended.reshape(NODES, D), gain_out)
    return jnp.dot(renormed, w_out, preferred_element_type=jnp.float32).astype(jnp.bfloat16)
```

```python
import functools

import jax
import jax.numpy as jnp
from jax import lax
from jax.experimental import pallas as pl
from jax.experimental.pallas import tpu as pltpu
from jax.sharding import PartitionSpec as P

D = 512
HEADS = 8
HW = D // HEADS
BLOCK = 64
NADJ = 7
BLK = 16
ROWS = BLK * BLOCK
CN = 20
CBLK = 40
WIN = 5 * BLK
NB = WIN + CBLK
CHUNK = 256
NCH = ROWS // CHUNK
CPAD = 48
GRP = 4
LOG_CAP = 60.0
BF = jnp.bfloat16
F32 = jnp.float32
I32 = jnp.int32
MESH = pl.DeviceIdType.MESH
NT = (((1,), (1,)), ((), ()))
neg_large = -1e30


def rms(vals, gain):
    mean_square = jnp.mean(vals * vals, axis=-1, keepdims=True)
    return (vals * lax.rsqrt(mean_square + 1e-06) * gain).astype(BF)


def place(x, y, z, c):
    return (lax.rem(z, 2) * 4 + y, (z // 2) * 8 + x * 2 + c)


def gather_kernel(
    feats, gain, w, src, adj, fine, mask,
    q_out, kv_out, list_out, stat_out,
    normed, nbr, picked, half, ag, kv, q_buf, lists, stats,
    send_n, recv_n, relay_send, a_sem, b_send, b_recv, c_send, c_recv, d_send, d_recv, e_send, e_recv,
    out_sem, misc_sem,
):
    r = lax.axis_index("region")
    s = lax.axis_index("sub")
    z_lo, y = r // 4, lax.rem(r, 4)
    z_hi, x, c = s // 8, lax.rem(s // 2, 4), lax.rem(s, 2)
    z = z_hi * 2 + z_lo
    me = r * 16 + s
    has = [r > 0, r < 7, s > 0, s < 15]
    partner = (r, s + 1 - 2 * c)
    y_next, y_prev, y_far = (place(x, lax.rem(y + k, 4), z, c) for k in (1, 3, 2))
    z_next, z_prev = (place(x, y, lax.rem(z + k, 4), c) for k in (1, 3))
    x_next, x_prev = (place(lax.rem(x + k, 4), y, z, c) for k in (1, 3))
    nbr_dev = [(r - 1, s), (r + 1, s), (r, s - 1), (r, s + 1)]

    for d in range(4):

        @pl.when(jnp.logical_not(has[d]))
        def _():
            nbr[d] = jnp.zeros((ROWS, D), BF)

    barrier = pltpu.get_barrier_semaphore()
    for dev in (partner, y_next, y_prev, y_far, z_next, z_prev, x_next, x_prev):
        pl.semaphore_signal(barrier, inc=1, device_id=dev, device_id_type=MESH)
    for d in range(4):

        @pl.when(has[d])
        def _():
            pl.semaphore_signal(barrier, inc=1, device_id=nbr_dev[d], device_id_type=MESH)

    src_row = (src[...] - me * ROWS).astype(F32)
    rows32 = lax.broadcasted_iota(I32, (32, CN), 0)
    cols32 = lax.broadcasted_iota(I32, (32, CN), 1)
    src_col = jnp.sum(jnp.where(rows32 == cols32, src_row, 0.0), axis=1, keepdims=True).astype(I32)
    hot = (lax.broadcasted_iota(I32, (32, ROWS), 1) == src_col).astype(BF)
    mine = rms(jnp.dot(hot, feats[...], preferred_element_type=F32), gain[...])
    picked[0] = mine[:, : D // 2]
    picked[1] = mine[:, D // 2 :]

    n_near = 8 + sum(h.astype(I32) for h in has)
    pl.semaphore_wait(barrier, n_near)

    def copy(src_ref, dst_ref, ss, rs, dev):
        return pltpu.make_async_remote_copy(
            src_ref=src_ref, dst_ref=dst_ref, send_sem=ss, recv_sem=rs, device_id=dev, device_id_type=MESH
        )

    a_copy = copy(picked.at[1 - c], half, a_sem.at[0], a_sem.at[1], partner)
    a_copy.start()

    def send_side(d, ch, dev, slot=None):
        slot = d ^ 1 if slot is None else slot
        rows = pl.ds(pl.multiple_of(ch * CHUNK, CHUNK), CHUNK)
        return copy(normed.at[rows], nbr.at[slot, rows], send_n.at[d, ch], recv_n.at[slot, ch], dev)

    def relay_side(d, ch, dev):
        rows = pl.ds(pl.multiple_of(ch * CHUNK, CHUNK), CHUNK)
        return copy(nbr.at[d, rows], nbr.at[d ^ 1, rows], relay_send.at[ch - 2], recv_n.at[d ^ 1, ch], dev)

    def side_to(d, ch):
        if d >= 2:
            return nbr_dev[d], d ^ 1
        turn = ((r == 4) if d == 0 else (r == 3)) & (ch >= 2)
        far = 0 if d == 0 else 7
        return (jnp.where(turn, far, nbr_dev[d][0]), s), jnp.where(turn, d, d ^ 1)

    def start_sides(dirs, ch):
        for d in dirs:

            @pl.when(has[d])
            def _():
                send_side(d, ch, *side_to(d, ch)).start()

    def norm_chunk(i, carry):
        ch = lax.rem(i + 2, NCH)
        rows = pl.ds(pl.multiple_of(ch * CHUNK, CHUNK), CHUNK)
        normed[rows] = rms(feats[rows].astype(F32), gain[...])
        start_sides((0, 1), ch)
        return carry

    lax.fori_loop(0, NCH, norm_chunk, 0)

    a_copy.wait()
    r48 = lax.broadcasted_iota(I32, (CPAD, 64), 0)
    c48 = lax.broadcasted_iota(I32, (CPAD, 64), 1)
    first = r48 < CN
    pick = jnp.where(first, r48, r48 + 12) == c48
    pick = (pick & (r48 < 2 * CN)).astype(BF)
    own_half = picked[c]
    lo = jnp.where(c == 0, own_half, half[...])
    hi = jnp.where(c == 0, half[...], own_half)
    ag[c, x, z, y] = jnp.dot(pick, jnp.concatenate([lo, hi], axis=0), preferred_element_type=F32).astype(BF)

    blk_ref = ag.at[c, x, z, y]
    b_copies = [copy(blk_ref, blk_ref, b_send.at[i], b_recv.at[i], dev) for i, dev in enumerate((y_next, y_prev, y_far))]
    for b in b_copies:
        b.start()

    heads_of = (lax.broadcasted_iota(I32, (D, 128), 0) // HW == lax.broadcasted_iota(I32, (D, 128), 1)).astype(BF)
    stats[...] = jnp.zeros_like(stats)

    def top_norm(vals):
        sq = (vals.astype(F32) * vals.astype(F32)).astype(BF)
        sums = jnp.dot(sq, heads_of, preferred_element_type=F32)
        return jnp.max(sums, axis=0, keepdims=True)

    def put_kv(vals, block, count, sem):
        kv[pl.ds(block, count)] = vals.reshape(count, BLOCK, 2 * D)
        stats[0:1] = jnp.maximum(stats[0:1], top_norm(vals[:, :D]))
        pltpu.make_async_copy(kv.at[pl.ds(block, count)], kv_out.at[pl.ds(block, count)], out_sem.at[sem]).start()

    def own_chunk(ch):
        rows = slice(ch * CHUNK, (ch + 1) * CHUNK)
        vals = normed[rows]
        qv = jnp.dot(vals, w[:, :D], preferred_element_type=F32).astype(BF) * jnp.asarray(HW**-0.5, BF)
        q_buf[rows] = qv
        stats[1:2] = jnp.maximum(stats[1:2], top_norm(qv))
        kvv = jnp.dot(vals, w[:, D:], preferred_element_type=F32).astype(BF)
        put_kv(kvv, 4 * ch, 4, ch)

    own_chunk(0)
    for b in b_copies:
        b.wait()

    def ring(slab, at, nxt, prv, snd, rcv, early, late):
        prev_at, next_at, far_at = (lax.rem(at + k, 4) for k in (3, 1, 2))
        to_next = [copy(slab(at, h), slab(at, h), snd.at[0, h], rcv.at[0, h], nxt) for h in range(2)]
        to_prev = [copy(slab(at, h), slab(at, h), snd.at[1, h], rcv.at[1, h], prv) for h in range(2)]
        for a in (to_next[0], to_prev[1], to_next[1], to_prev[0]):
            a.start()
        early()
        to_next[0].wait_recv()
        on_next = copy(slab(prev_at, 0), slab(prev_at, 0), snd.at[2, 0], rcv.at[2, 0], nxt)
        on_next.start()
        to_prev[1].wait_recv()
        on_prev = copy(slab(next_at, 1), slab(next_at, 1), snd.at[2, 1], rcv.at[2, 1], prv)
        on_prev.start()
        to_next[1].wait_recv()
        to_prev[0].wait_recv()
        late(prev_at, next_at)
        on_next.wait_recv()
        on_prev.wait_recv()
        for a in to_next + to_prev + [on_next, on_prev]:
            a.wait_send()
        return far_at

    ring(
        lambda i, h: ag.at[c, x, i, pl.ds(2 * h, 2)], z, z_next, z_prev, c_send, c_recv,
        lambda: own_chunk(1), lambda p, n: None,
    )

    def e_copy(i):
        return copy(ag.at[c, i], ag.at[c, i], e_send.at[i], e_recv.at[i], partner)

    def e_start(i):
        e_copy(i).start()

    def d_early():
        e_start(x)

        def sides(i, carry):
            start_sides((2, 3), lax.rem(i + 2, NCH))
            return carry

        lax.fori_loop(0, NCH, sides, 0)
        own_chunk(2)
        own_chunk(3)
        q_copy = pltpu.make_async_copy(q_buf, q_out, misc_sem.at[0])
        q_copy.start()
        dev_of, local = adj[...] // BLK, lax.rem(adj[...], BLK)
        gap = dev_of - me
        side = jnp.where(gap == -16, 1, jnp.where(gap == 16, 2, jnp.where(gap == -1, 3, jnp.where(gap == 1, 4, 0))))
        slot = side * BLK + local
        fine_live = (fine[...] == 1) | (lax.broadcasted_iota(I32, (BLK, NADJ), 1) == 0)
        fine_n = fine_live.astype(I32)
        coarse_n = (mask[...] == 1).astype(I32)
        spot = lax.broadcasted_iota(I32, (BLK, 128), 1)
        found = jnp.full((BLK, 128), NB, I32)
        count = jnp.zeros((BLK, 1), I32)
        for j in range(CBLK):
            live = coarse_n[:, j : j + 1]
            found = jnp.where(spot == jnp.where(live == 1, count, -1), WIN + j, found)
            count = count + live
        for j in range(NADJ):
            live = fine_n[:, j : j + 1]
            found = jnp.where(spot == jnp.where(live == 1, count, -1), slot[:, j : j + 1], found)
            count = count + live
        lists[...] = jnp.where(spot == 127, count, found)
        pltpu.make_async_copy(lists, list_out, misc_sem.at[1]).start()

    def d_late(p, n):
        e_start(p)
        e_start(n)
        relay = [(7, 1, 4), (0, 0, 3)]
        for at, d, to in relay:

            @pl.when(r == at)
            def _():
                for ch in (2, 3):
                    side = send_side(d ^ 1, ch, (to, s))
                    side.wait_recv()
                    relay_side(d, ch, (to, s)).start()

    far = ring(
        lambda i, h: ag.at[c, i, pl.ds(2 * h, 2)], x, x_next, x_prev, d_send, d_recv, d_early, d_late
    )
    e_start(far)

    def e_wait(i, carry):
        e_copy(i).wait()
        return carry

    lax.fori_loop(0, 4, e_wait, 0)

    r160 = lax.broadcasted_iota(I32, (160, 4 * CPAD), 0)
    c160 = lax.broadcasted_iota(I32, (160, 4 * CPAD), 1)
    sel = ((r160 // 40) * CPAD + lax.rem(r160, 40) == c160).astype(BF)

    def coarse_part(i, carry):
        zl, yy = i // 4, lax.rem(i, 4)
        parts = []
        for zh in range(2):
            zz = zh * 2 + zl
            cols = []
            for h in range(2):
                got = jnp.concatenate([ag[h, k, zz, yy] for k in range(4)], axis=0)
                cols.append(jnp.dot(sel, got, preferred_element_type=F32).astype(BF))
            parts.append(jnp.concatenate(cols, axis=1))
        vals = jnp.concatenate(parts, axis=0)
        put_kv(jnp.dot(vals, w[:, D:], preferred_element_type=F32).astype(BF), WIN + 5 * i, 5, 20 + i)
        return carry

    lax.fori_loop(0, 8, coarse_part, 0)

    def side_part(i, carry):
        ch = lax.rem(i + 2, NCH)
        for d in (2, 3, 0, 1):

            @pl.when(has[d])
            def _():
                send_side(d ^ 1, ch, nbr_dev[d]).wait_recv()

            rows = pl.ds(pl.multiple_of(ch * CHUNK, CHUNK), CHUNK)
            vals = jnp.dot(nbr[d, rows], w[:, D:], preferred_element_type=F32).astype(BF)
            put_kv(vals, (d + 1) * BLK + 4 * ch, 4, 4 + d * 4 + ch)
        return carry

    lax.fori_loop(0, NCH, side_part, 0)

    stat_copy = pltpu.make_async_copy(stats, stat_out, misc_sem.at[2])
    stat_copy.start()

    def send_wait(ch, carry):
        for d in range(4):

            @pl.when(has[d])
            def _():
                send_side(d, ch, nbr_dev[d]).wait_send()

        return carry

    lax.fori_loop(0, NCH, send_wait, 0)
    for at, d, to in ((7, 1, 4), (0, 0, 3)):

        @pl.when(r == at)
        def _():
            for ch in (2, 3):
                relay_side(d, ch, (to, s)).wait_send()

    def out_wait(i, carry):
        pltpu.make_async_copy(kv.at[pl.ds(4 * i, 4)], kv_out.at[pl.ds(4 * i, 4)], out_sem.at[i]).wait()
        return carry

    def out_wait_c(i, carry):
        at = pl.ds(WIN + 5 * i, 5)
        pltpu.make_async_copy(kv.at[at], kv_out.at[at], out_sem.at[20 + i]).wait()
        return carry

    lax.fori_loop(0, 20, out_wait, 0)
    lax.fori_loop(0, 8, out_wait_c, 0)
    pltpu.make_async_copy(q_buf, q_out, misc_sem.at[0]).wait()
    pltpu.make_async_copy(lists, list_out, misc_sem.at[1]).wait()
    stat_copy.wait()


def attend_kernel(unroll, lists, q_hbm, kv_hbm, stats, gain, w, out, q, kv, qm, acc, lsum, sems):
    q_copy = pltpu.make_async_copy(q_hbm, q, sems.at[0])
    kv_copy = pltpu.make_async_copy(kv_hbm, kv.at[pl.ds(0, NB)], sems.at[1])
    q_copy.start()
    kv_copy.start()
    lane = lax.broadcasted_iota(I32, (BLOCK, 256), 1) // HW
    zero = jnp.zeros((), BF)
    acc[...] = jnp.zeros_like(acc)
    lsum[...] = jnp.zeros_like(lsum)
    kv[NB] = jnp.zeros((BLOCK, 2 * D), BF)
    qm[BLK] = jnp.zeros((2, 256, 256), BF)
    q_copy.wait()

    def spread(b, carry):
        rows = pl.ds(pl.multiple_of(b * BLOCK, BLOCK), BLOCK)
        for g in range(2):
            qb = q[rows, g * 256 : (g + 1) * 256]
            for h in range(4):
                qm[b, g, h * BLOCK : (h + 1) * BLOCK, :] = jnp.where(lane == h, qb, zero)
        return carry

    lax.fori_loop(0, BLK, spread, 0)
    kv_copy.wait()

    bound = jnp.max(jnp.sqrt(stats[0:1]) * jnp.sqrt(stats[1:2])) * 1.02
    safe = bound < LOG_CAP

    def groups(b):
        return jnp.where(b < BLK, (lists[jnp.minimum(b, BLK - 1), 127] + GRP - 1) // GRP, 0)

    def blocks_of(b, t, lo):
        bb = jnp.minimum(b, BLK - 1)
        return jnp.concatenate([kv[lists[bb, t * GRP + j], :, lo : lo + 256] for j in range(GRP)], axis=0)

    def scores(b, t, g):
        return lax.dot_general(qm[b, g], blocks_of(b, t, g * 256), NT, preferred_element_type=F32)

    key_lane = lax.broadcasted_iota(I32, (1, 256), 1)

    def open_keys(b, t):
        bb = jnp.minimum(b, BLK - 1)
        return key_lane < (lists[bb, 127] - t * GRP) * BLOCK

    def add_up(b, t, g, p, keys):
        kept = jnp.where(keys, p, 0.0)
        lsum[b, g] += kept[:, :128] + kept[:, 128:]
        acc[b, g] += jnp.dot(p.astype(BF), blocks_of(b, t, D + g * 256), preferred_element_type=F32)

    @pl.when(safe)
    def _():
        total = functools.reduce(lambda a, b: a + b, [groups(b) for b in range(BLK)])

        def step_on(b, t):
            last = t + 1 >= groups(b)
            return jnp.where(last, jnp.minimum(b + 1, BLK), b), jnp.where(last, 0, t + 1)

        def body(i, at):
            spots = [at]
            for _ in range(unroll):
                spots.append(step_on(*spots[-1]))
            held = [scores(*spots[0], g) for g in range(2)]
            for u in range(unroll):
                later = [scores(*spots[u + 1], g) for g in range(2)] if u + 1 < unroll else None
                keys = open_keys(*spots[u])
                for g in range(2):
                    add_up(*spots[u], g, jnp.exp(held[g]), keys)
                held = later
            return spots[-1]

        lax.fori_loop(0, (total + unroll - 1) // unroll, body, (jnp.int32(0), jnp.int32(0)))

    @pl.when(jnp.logical_not(safe))
    def _():
        def block(b, carry):
            for g in range(2):
                def peak(t, m):
                    sc = jnp.where(open_keys(b, t), scores(b, t, g), neg_large)
                    return jnp.maximum(m, jnp.max(sc, axis=-1, keepdims=True))

                top = lax.fori_loop(0, groups(b), peak, jnp.full((256, 1), neg_large, F32))

                def weigh(t, carry):
                    keys = open_keys(b, t)
                    sc = jnp.where(keys, scores(b, t, g), neg_large)
                    add_up(b, t, g, jnp.exp(sc - top), keys)
                    return carry

                lax.fori_loop(0, groups(b), weigh, 0)
            return carry

        lax.fori_loop(0, BLK, block, 0)

    def finish(b, carry):
        pieces = []
        for g in range(2):
            piece = jnp.zeros((BLOCK, 256), F32)
            for h in range(4):
                rows = slice(h * BLOCK, (h + 1) * BLOCK)
                total = jnp.sum(lsum[b, g, rows, :], axis=-1, keepdims=True)
                piece = jnp.where(lane == h, acc[b, g, rows, :] / total, piece)
            pieces.append(piece)
        attended = jnp.concatenate(pieces, axis=1).astype(BF).astype(F32)
        rows = pl.ds(pl.multiple_of(b * BLOCK, BLOCK), BLOCK)
        q[rows] = rms(attended, gain[...])
        return carry

    lax.fori_loop(0, BLK, finish, 0)
    for i in range(4):
        rows = slice(i * CHUNK, (i + 1) * CHUNK)
        out[rows] = jnp.dot(q[rows], w[...], preferred_element_type=F32).astype(BF)


def per_device(node_feats, gain_in, w_qkv, gain_out, w_out, adjacency, fine_valid, coarse_mask, coarse_src):
    vmem = pl.BlockSpec(memory_space=pltpu.VMEM)
    anywhere = pl.BlockSpec(memory_space=pl.ANY)
    dma = pltpu.SemaphoreType.DMA
    q, kv, lists, stats = pl.pallas_call(
        gather_kernel,
        out_shape=(
            jax.ShapeDtypeStruct((ROWS, D), BF),
            jax.ShapeDtypeStruct((NB, BLOCK, 2 * D), BF),
            jax.ShapeDtypeStruct((BLK, 128), I32),
            jax.ShapeDtypeStruct((8, 128), F32),
        ),
        in_specs=[vmem] * 7,
        out_specs=(anywhere,) * 4,
        scratch_shapes=[
            pltpu.VMEM((ROWS, D), BF),
            pltpu.VMEM((4, ROWS, D), BF),
            pltpu.VMEM((2, 32, D // 2), BF),
            pltpu.VMEM((32, D // 2), BF),
            pltpu.VMEM((2, 4, 4, 4, CPAD, D // 2), BF),
            pltpu.VMEM((NB, BLOCK, 2 * D), BF),
            pltpu.VMEM((ROWS, D), BF),
            pltpu.VMEM((BLK, 128), I32),
            pltpu.VMEM((8, 128), F32),
            dma((4, 4)), dma((4, 4)), dma((2,)), dma((2,)), dma((3,)), dma((3,)),
            dma((3, 2)), dma((3, 2)), dma((3, 2)), dma((3, 2)), dma((4,)), dma((4,)),
            dma((28,)), dma((3,)),
        ],
        compiler_params=pltpu.CompilerParams(
            collective_id=0, has_side_effects=True, vmem_limit_bytes=48 * 2**20
        ),
    )(
        node_feats, gain_in.reshape(1, D), w_qkv, coarse_src.reshape(1, CN),
        adjacency, fine_valid, coarse_mask,
    )
    smem = pl.BlockSpec(memory_space=pltpu.SMEM)
    return pl.pallas_call(
        functools.partial(attend_kernel, 8),
        out_shape=jax.ShapeDtypeStruct((ROWS, D), BF),
        in_specs=[smem, anywhere, anywhere, vmem, vmem, vmem],
        out_specs=vmem,
        scratch_shapes=[
            pltpu.VMEM((ROWS, D), BF),
            pltpu.VMEM((NB + 1, BLOCK, 2 * D), BF),
            pltpu.VMEM((BLK + 1, 2, 256, 256), BF),
            pltpu.VMEM((BLK + 1, 2, 256, 256), F32),
            pltpu.VMEM((BLK + 1, 2, 256, 128), F32),
            dma((2,)),
        ],
        compiler_params=pltpu.CompilerParams(vmem_limit_bytes=56 * 2**20),
    )(lists, q, kv, stats, gain_out.reshape(1, D), w_out)


def solution(mesh):
    both = ("region", "sub")
    in_specs = (P(both, None), P(), P(), P(), P(), P(both, None), P(both, None), P(both, None), P(both))
    return jax.shard_map(per_device, mesh=mesh, in_specs=in_specs, out_specs=P(both, None), check_vma=False)
```

```python
import functools

import jax
import jax.numpy as jnp
from jax import lax
from jax.experimental import pallas as pl
from jax.experimental.pallas import tpu as pltpu
from jax.sharding import PartitionSpec as P

D = 512
HEADS = 8
HW = D // HEADS
BLOCK = 64
NADJ = 7
BLK = 16
ROWS = BLK * BLOCK
CN = 20
CBLK = 40
WIN = 5 * BLK
NB = WIN + CBLK
CHUNK = 256
NCH = ROWS // CHUNK
CPAD = 48
GRP = 4
LOG_CAP = 60.0
EARLY_X = ()
LATE_X = (2, 3, 0, 1)
BF = jnp.bfloat16
F32 = jnp.float32
I32 = jnp.int32
MESH = pl.DeviceIdType.MESH
NT = (((1,), (1,)), ((), ()))
neg_large = -1e30


def rms(vals, gain):
    mean_square = jnp.mean(vals * vals, axis=-1, keepdims=True)
    return (vals * lax.rsqrt(mean_square + 1e-06) * gain).astype(BF)


def place(x, y, z, c):
    return (lax.rem(z, 2) * 4 + y, (z // 2) * 8 + x * 2 + c)


def gather_kernel(
    feats_hbm, gain_hbm, w_hbm, src_hbm, adj_hbm, fine_hbm, mask_hbm,
    qm, kv, lists, stats,
    feats, gain, w, src, adj, fine, mask, normed, nbr, picked, half, ag,
    send_n, recv_n, relay_send, a_sem, b_send, b_recv, c_send, c_recv, d_send, d_recv, e_send, e_recv, in_sem,
):
    r = lax.axis_index("region")
    s = lax.axis_index("sub")
    z_lo, y = r // 4, lax.rem(r, 4)
    z_hi, x, c = s // 8, lax.rem(s // 2, 4), lax.rem(s, 2)
    z = z_hi * 2 + z_lo
    me = r * 16 + s
    has = [r > 0, r < 7, s > 0, s < 15]
    partner = (r, s + 1 - 2 * c)
    y_next, y_prev, y_far = (place(x, lax.rem(y + k, 4), z, c) for k in (1, 3, 2))
    z_next, z_prev = (place(x, y, lax.rem(z + k, 4), c) for k in (1, 3))
    x_next, x_prev = (place(lax.rem(x + k, 4), y, z, c) for k in (1, 3))
    nbr_dev = [(r - 1, s), (r + 1, s), (r, s - 1), (r, s + 1)]

    loads = [
        pltpu.make_async_copy(a, b, in_sem.at[i])
        for i, (a, b) in enumerate(
            ((src_hbm, src), (gain_hbm, gain), (feats_hbm, feats), (w_hbm, w), (adj_hbm, adj), (fine_hbm, fine), (mask_hbm, mask))
        )
    ]
    for load in loads:
        load.start()

    for d in range(4):

        @pl.when(jnp.logical_not(has[d]))
        def _():
            nbr[d] = jnp.zeros((ROWS, D), BF)

    barrier = pltpu.get_barrier_semaphore()
    for dev in (partner, y_next, y_prev, y_far, z_next, z_prev, x_next, x_prev):
        pl.semaphore_signal(barrier, inc=1, device_id=dev, device_id_type=MESH)
    for d in range(4):

        @pl.when(has[d])
        def _():
            pl.semaphore_signal(barrier, inc=1, device_id=nbr_dev[d], device_id_type=MESH)

    for load in loads[:3]:
        load.wait()
    src_row = (src[...] - me * ROWS).astype(F32)
    rows32 = lax.broadcasted_iota(I32, (32, CN), 0)
    cols32 = lax.broadcasted_iota(I32, (32, CN), 1)
    src_col = jnp.sum(jnp.where(rows32 == cols32, src_row, 0.0), axis=1, keepdims=True).astype(I32)
    hot = (lax.broadcasted_iota(I32, (32, ROWS), 1) == src_col).astype(BF)
    mine = rms(jnp.dot(hot, feats[...], preferred_element_type=F32), gain[...])
    picked[0] = mine[:, : D // 2]
    picked[1] = mine[:, D // 2 :]

    n_near = 8 + sum(h.astype(I32) for h in has)
    pl.semaphore_wait(barrier, n_near)

    def copy(src_ref, dst_ref, ss, rs, dev):
        return pltpu.make_async_remote_copy(
            src_ref=src_ref, dst_ref=dst_ref, send_sem=ss, recv_sem=rs, device_id=dev, device_id_type=MESH
        )

    a_copy = copy(picked.at[1 - c], half, a_sem.at[0], a_sem.at[1], partner)
    a_copy.start()

    def send_side(d, ch, dev, slot=None):
        slot = d ^ 1 if slot is None else slot
        rows = pl.ds(pl.multiple_of(ch * CHUNK, CHUNK), CHUNK)
        return copy(normed.at[rows], nbr.at[slot, rows], send_n.at[d, ch], recv_n.at[slot, ch], dev)

    def relay_side(d, ch, dev):
        rows = pl.ds(pl.multiple_of(ch * CHUNK, CHUNK), CHUNK)
        return copy(nbr.at[d, rows], nbr.at[d ^ 1, rows], relay_send.at[ch - 2], recv_n.at[d ^ 1, ch], dev)

    def side_to(d, ch):
        if d >= 2:
            return nbr_dev[d], d ^ 1
        turn = ((r == 4) if d == 0 else (r == 3)) & (ch >= 2)
        far = 0 if d == 0 else 7
        return (jnp.where(turn, far, nbr_dev[d][0]), s), jnp.where(turn, d, d ^ 1)

    def start_sides(dirs, ch, crossing=None):
        for d in dirs:
            now = has[d]
            if crossing is not None:
                over = (r == 4) if d == 0 else (r == 3)
                now = now & (over if crossing else jnp.logical_not(over))

            @pl.when(now)
            def _():
                send_side(d, ch, *side_to(d, ch)).start()

    def norm_chunk(ch):
        rows = pl.ds(ch * CHUNK, CHUNK)
        normed[rows] = rms(feats[rows].astype(F32), gain[...])

    norm_chunk(2)
    a_copy.wait()
    r48 = lax.broadcasted_iota(I32, (CPAD, 64), 0)
    c48 = lax.broadcasted_iota(I32, (CPAD, 64), 1)
    first = r48 < CN
    pick = jnp.where(first, r48, r48 + 12) == c48
    pick = (pick & (r48 < 2 * CN)).astype(BF)
    own_half = picked[c]
    lo = jnp.where(c == 0, own_half, half[...])
    hi = jnp.where(c == 0, half[...], own_half)
    ag[c, x, z, y] = jnp.dot(pick, jnp.concatenate([lo, hi], axis=0), preferred_element_type=F32).astype(BF)

    blk_ref = ag.at[c, x, z, y]
    b_copies = [copy(blk_ref, blk_ref, b_send.at[i], b_recv.at[i], dev) for i, dev in enumerate((y_next, y_prev, y_far))]
    for b in b_copies:
        b.start()
    for ch in (3, 0, 1):
        norm_chunk(ch)
    for load in loads[3:]:
        load.wait()

    heads_of = (lax.broadcasted_iota(I32, (D, 128), 0) // HW == lax.broadcasted_iota(I32, (D, 128), 1)).astype(BF)
    stats[...] = jnp.zeros_like(stats)

    def top_norm(vals):
        sq = (vals.astype(F32) * vals.astype(F32)).astype(BF)
        sums = jnp.dot(sq, heads_of, preferred_element_type=F32)
        return jnp.max(sums, axis=0, keepdims=True)

    def put_kv(vals, block, count):
        kv[pl.ds(block, count)] = vals.reshape(count, BLOCK, 2 * D)
        stats[0:1] = jnp.maximum(stats[0:1], top_norm(vals[:, :D]))

    lane_head = lax.broadcasted_iota(I32, (CHUNK, 256), 1) // HW

    def own_chunk(ch):
        vals = normed[pl.ds(ch * CHUNK, CHUNK)]
        qv = jnp.dot(vals, w[:, :D], preferred_element_type=F32).astype(BF) * jnp.asarray(HW**-0.5, BF)
        stats[1:2] = jnp.maximum(stats[1:2], top_norm(qv))
        for g in range(2):
            for h in range(4):
                qh = jnp.where(lane_head == h, qv[:, g * 256 : (g + 1) * 256], jnp.zeros((), BF))
                qm[pl.ds(4 * ch, 4), g, h * BLOCK : (h + 1) * BLOCK, :] = qh.reshape(4, BLOCK, 256)
        put_kv(jnp.dot(vals, w[:, D:], preferred_element_type=F32).astype(BF), 4 * ch, 4)

    for b in b_copies:
        b.wait()

    def side_part(ch, dirs):
        for d in dirs:

            @pl.when(has[d])
            def _():
                send_side(d ^ 1, ch, nbr_dev[d]).wait_recv()

            rows = pl.ds(pl.multiple_of(ch * CHUNK, CHUNK), CHUNK)
            vals = jnp.dot(nbr[d, rows], w[:, D:], preferred_element_type=F32).astype(BF)
            put_kv(vals, (d + 1) * BLK + 4 * ch, 4)

    def ring(slab, at, nxt, prv, snd, rcv, early, late):
        prev_at, next_at, far_at = (lax.rem(at + k, 4) for k in (3, 1, 2))
        to_next = [copy(slab(at, h), slab(at, h), snd.at[0, h], rcv.at[0, h], nxt) for h in range(2)]
        to_prev = [copy(slab(at, h), slab(at, h), snd.at[1, h], rcv.at[1, h], prv) for h in range(2)]
        for a in (to_next[0], to_prev[1], to_next[1], to_prev[0]):
            a.start()
        early()
        to_next[0].wait_recv()
        on_next = copy(slab(prev_at, 0), slab(prev_at, 0), snd.at[2, 0], rcv.at[2, 0], nxt)
        on_next.start()
        to_prev[1].wait_recv()
        on_prev = copy(slab(next_at, 1), slab(next_at, 1), snd.at[2, 1], rcv.at[2, 1], prv)
        on_prev.start()
        to_next[1].wait_recv()
        to_prev[0].wait_recv()
        late(prev_at, next_at)
        on_next.wait_recv()
        on_prev.wait_recv()
        for a in to_next + to_prev + [on_next, on_prev]:
            a.wait_send()
        return far_at

    def c_early():
        def sides(i, carry):
            start_sides((0, 1), lax.rem(i + 2, NCH), False)
            return carry

        lax.fori_loop(0, NCH, sides, 0)
        own_chunk(0)

    ring(
        lambda i, h: ag.at[c, x, i, pl.ds(2 * h, 2)], z, z_next, z_prev, c_send, c_recv,
        c_early, lambda p, n: None,
    )

    def e_copy(i):
        return copy(ag.at[c, i], ag.at[c, i], e_send.at[i], e_recv.at[i], partner)

    def e_start(i):
        e_copy(i).start()

    def d_early():
        e_start(x)

        def sides(i, carry):
            start_sides((0, 1), lax.rem(i + 2, NCH), True)
            return carry

        lax.fori_loop(0, NCH, sides, 0)
        for ch in EARLY_X:
            start_sides((2, 3), ch)
        own_chunk(1)
        own_chunk(2)
        own_chunk(3)
        dev_of, local = adj[...] // BLK, lax.rem(adj[...], BLK)
        gap = dev_of - me
        side = jnp.where(gap == -16, 1, jnp.where(gap == 16, 2, jnp.where(gap == -1, 3, jnp.where(gap == 1, 4, 0))))
        slot = side * BLK + local
        fine_live = (fine[...] == 1) | (lax.broadcasted_iota(I32, (NADJ, BLK), 0) == 0)
        fine_n = fine_live.astype(I32)
        eye = (lax.broadcasted_iota(I32, (BLK, BLK), 0) == lax.broadcasted_iota(I32, (BLK, BLK), 1)).astype(BF)
        coarse_n = lax.dot_general(
            (mask[...] == 1).astype(BF), eye, (((0,), (0,)), ((), ())), preferred_element_type=F32
        ).astype(I32)
        spot = lax.broadcasted_iota(I32, (56, BLK), 0)
        found = jnp.full((56, BLK), NB, I32)
        count = jnp.zeros((1, BLK), I32)
        for j in range(CBLK):
            live = coarse_n[j : j + 1]
            found = jnp.where(spot == jnp.where(live == 1, count, -1), WIN + j, found)
            count = count + live
        for j in range(NADJ):
            live = fine_n[j : j + 1]
            found = jnp.where(spot == jnp.where(live == 1, count, -1), slot[j : j + 1], found)
            count = count + live
        lists[...] = jnp.zeros_like(lists)
        lists[:, :BLK] = jnp.where(spot == 48, count, found)
        kv[NB] = jnp.zeros((BLOCK, 2 * D), BF)

    def d_late(p, n):
        e_start(p)
        e_start(n)
        for ch in LATE_X:
            start_sides((2, 3), ch)
        relay = [(7, 1, 4), (0, 0, 3)]
        for at, d, to in relay:

            @pl.when(r == at)
            def _():
                for ch in (2, 3):
                    side = send_side(d ^ 1, ch, (to, s))
                    side.wait_recv()
                    relay_side(d, ch, (to, s)).start()

    far = ring(
        lambda i, h: ag.at[c, i, pl.ds(2 * h, 2)], x, x_next, x_prev, d_send, d_recv, d_early, d_late
    )
    e_start(far)
    side_part(2, (0, 1))

    def e_wait(i, carry):
        e_copy(i).wait()
        return carry

    lax.fori_loop(0, 4, e_wait, 0)

    r160 = lax.broadcasted_iota(I32, (160, 4 * CPAD), 0)
    c160 = lax.broadcasted_iota(I32, (160, 4 * CPAD), 1)
    sel = ((r160 // 40) * CPAD + lax.rem(r160, 40) == c160).astype(BF)

    def coarse_part(i, carry):
        zl, yy = i // 4, lax.rem(i, 4)
        parts = []
        for zh in range(2):
            zz = zh * 2 + zl
            cols = []
            for h in range(2):
                got = jnp.concatenate([ag[h, k, zz, yy] for k in range(4)], axis=0)
                cols.append(jnp.dot(sel, got, preferred_element_type=F32).astype(BF))
            parts.append(jnp.concatenate(cols, axis=1))
        vals = jnp.concatenate(parts, axis=0)
        put_kv(jnp.dot(vals, w[:, D:], preferred_element_type=F32).astype(BF), WIN + 5 * i, 5)
        return carry

    lax.fori_loop(0, 8, coarse_part, 0)

    side_part(2, (2, 3))

    def rest(i, carry):
        side_part(lax.rem(i + 3, NCH), (0, 1, 2, 3))
        return carry

    lax.fori_loop(0, NCH - 1, rest, 0)

    def send_wait(ch, carry):
        for d in range(4):

            @pl.when(has[d])
            def _():
                send_side(d, ch, nbr_dev[d]).wait_send()

        return carry

    lax.fori_loop(0, NCH, send_wait, 0)
    for at, d, to in ((7, 1, 4), (0, 0, 3)):

        @pl.when(r == at)
        def _():
            for ch in (2, 3):
                relay_side(d, ch, (to, s)).wait_send()


def attend_kernel(unroll, lists_vmem, qm, kv, stats, gain_hbm, w_hbm, out, lists, gain, w, mid, acc, lsum, sems):
    loads = [
        pltpu.make_async_copy(a, b, sems.at[i])
        for i, (a, b) in enumerate(((lists_vmem, lists), (gain_hbm, gain), (w_hbm, w)))
    ]
    for load in loads:
        load.start()
    lane = lax.broadcasted_iota(I32, (BLOCK, 256), 1) // HW
    acc[...] = jnp.zeros_like(acc)
    lsum[...] = jnp.zeros_like(lsum)
    for load in loads:
        load.wait()

    bound = jnp.max(jnp.sqrt(stats[0:1]) * jnp.sqrt(stats[1:2])) * 1.02
    safe = bound < LOG_CAP

    def groups(b):
        return jnp.where(b < BLK, (lists[48, jnp.minimum(b, BLK - 1)] + GRP - 1) // GRP, 0)

    def blocks_of(b, t, lo):
        bb = jnp.minimum(b, BLK - 1)
        return jnp.concatenate([kv[lists[t * GRP + j, bb], :, lo : lo + 256] for j in range(GRP)], axis=0)

    def scores(b, t, g):
        return lax.dot_general(qm[jnp.minimum(b, BLK - 1), g], blocks_of(b, t, g * 256), NT, preferred_element_type=F32)

    key_lane = lax.broadcasted_iota(I32, (1, 256), 1)

    def open_keys(b, t):
        bb = jnp.minimum(b, BLK - 1)
        return key_lane < (lists[48, bb] - t * GRP) * BLOCK

    def add_up(b, t, g, p, keys):
        kept = jnp.where(keys, p, 0.0)
        lsum[b, g] += kept[:, :128] + kept[:, 128:]
        acc[b, g] += jnp.dot(p.astype(BF), blocks_of(b, t, D + g * 256), preferred_element_type=F32)

    @pl.when(safe)
    def _():
        total = functools.reduce(lambda a, b: a + b, [groups(b) for b in range(BLK)])

        def step_on(b, t):
            last = t + 1 >= groups(b)
            return jnp.where(last, jnp.minimum(b + 1, BLK), b), jnp.where(last, 0, t + 1)

        def body(i, at):
            spots = [at]
            for _ in range(unroll):
                spots.append(step_on(*spots[-1]))
            held = [scores(*spots[0], g) for g in range(2)]
            for u in range(unroll):
                later = [scores(*spots[u + 1], g) for g in range(2)] if u + 1 < unroll else None
                keys = open_keys(*spots[u])
                for g in range(2):
                    add_up(*spots[u], g, jnp.exp(held[g]), keys)
                held = later
            return spots[-1]

        lax.fori_loop(0, (total + unroll - 1) // unroll, body, (jnp.int32(0), jnp.int32(0)))

    @pl.when(jnp.logical_not(safe))
    def _():
        def block(b, carry):
            for g in range(2):
                def peak(t, m):
                    sc = jnp.where(open_keys(b, t), scores(b, t, g), neg_large)
                    return jnp.maximum(m, jnp.max(sc, axis=-1, keepdims=True))

                top = lax.fori_loop(0, groups(b), peak, jnp.full((256, 1), neg_large, F32))

                def weigh(t, carry):
                    keys = open_keys(b, t)
                    sc = jnp.where(keys, scores(b, t, g), neg_large)
                    add_up(b, t, g, jnp.exp(sc - top), keys)
                    return carry

                lax.fori_loop(0, groups(b), weigh, 0)
            return carry

        lax.fori_loop(0, BLK, block, 0)

    def finish(i, carry):
        for k in range(4):
            b = 4 * i + k
            pieces = []
            for g in range(2):
                piece = jnp.zeros((BLOCK, 256), F32)
                for h in range(4):
                    rows = slice(h * BLOCK, (h + 1) * BLOCK)
                    total = jnp.sum(lsum[b, g, rows, :], axis=-1, keepdims=True)
                    piece = jnp.where(lane == h, acc[b, g, rows, :] / total, piece)
                pieces.append(piece)
            attended = jnp.concatenate(pieces, axis=1).astype(BF).astype(F32)
            mid[k * BLOCK : (k + 1) * BLOCK] = rms(attended, gain[...])
        rows = pl.ds(pl.multiple_of(i * CHUNK, CHUNK), CHUNK)
        out[rows] = jnp.dot(mid[...], w[...], preferred_element_type=F32).astype(BF)
        return carry

    lax.fori_loop(0, 4, finish, 0)


def per_device(node_feats, gain_in, w_qkv, gain_out, w_out, adjacency, fine_valid, coarse_mask, coarse_src):
    vmem = pl.BlockSpec(memory_space=pltpu.VMEM)
    hbm = pl.BlockSpec(memory_space=pltpu.HBM)
    dma = pltpu.SemaphoreType.DMA
    qm, kv, lists, stats = pl.pallas_call(
        gather_kernel,
        out_shape=(
            jax.ShapeDtypeStruct((BLK, 2, 256, 256), BF),
            jax.ShapeDtypeStruct((NB + 1, BLOCK, 2 * D), BF),
            jax.ShapeDtypeStruct((56, 128), I32),
            jax.ShapeDtypeStruct((8, 128), F32),
        ),
        in_specs=[hbm] * 7,
        out_specs=(vmem,) * 4,
        scratch_shapes=[
            pltpu.VMEM((ROWS, D), BF),
            pltpu.VMEM((1, D), F32),
            pltpu.VMEM((D, 3 * D), BF),
            pltpu.VMEM((1, CN), I32),
            pltpu.VMEM((NADJ, BLK), I32),
            pltpu.VMEM((NADJ, BLK), I32),
            pltpu.VMEM((BLK, CBLK), I32),
            pltpu.VMEM((ROWS, D), BF),
            pltpu.VMEM((4, ROWS, D), BF),
            pltpu.VMEM((2, 32, D // 2), BF),
            pltpu.VMEM((32, D // 2), BF),
            pltpu.VMEM((2, 4, 4, 4, CPAD, D // 2), BF),
            dma((4, 4)), dma((4, 4)), dma((2,)), dma((2,)), dma((3,)), dma((3,)),
            dma((3, 2)), dma((3, 2)), dma((3, 2)), dma((3, 2)), dma((4,)), dma((4,)),
            dma((7,)),
        ],
        compiler_params=pltpu.CompilerParams(
            collective_id=0, has_side_effects=True, vmem_limit_bytes=24 * 2**20
        ),
    )(
        *(
            pltpu.with_memory_space_constraint(a, pltpu.HBM)
            for a in (
                node_feats, gain_in.reshape(1, D), w_qkv, coarse_src.reshape(1, CN),
                adjacency.T, fine_valid.T, coarse_mask,
            )
        )
    )
    return pl.pallas_call(
        functools.partial(attend_kernel, 8),
        out_shape=jax.ShapeDtypeStruct((ROWS, D), BF),
        in_specs=[vmem, vmem, vmem, vmem, hbm, hbm],
        out_specs=vmem,
        scratch_shapes=[
            pltpu.SMEM((56, 128), I32),
            pltpu.VMEM((1, D), F32),
            pltpu.VMEM((D, D), BF),
            pltpu.VMEM((CHUNK, D), BF),
            pltpu.VMEM((BLK + 1, 2, 256, 256), F32),
            pltpu.VMEM((BLK + 1, 2, 256, 128), F32),
            dma((3,)),
        ],
        compiler_params=pltpu.CompilerParams(vmem_limit_bytes=28 * 2**20),
    )(lists, qm, kv, stats, gain_out.reshape(1, D), w_out)


def solution(mesh):
    both = ("region", "sub")
    in_specs = (P(both, None), P(), P(), P(), P(), P(both, None), P(both, None), P(both, None), P(both))
    return jax.shard_map(per_device, mesh=mesh, in_specs=in_specs, out_specs=P(both, None), check_vma=False)
```

```python
import functools

import jax
import jax.numpy as jnp
from jax import lax
from jax.experimental import pallas as pl
from jax.experimental.pallas import tpu as pltpu
from jax.sharding import PartitionSpec as P

D = 512
HEADS = 8
HW = D // HEADS
BLOCK = 64
NADJ = 7
BLK = 16
ROWS = BLK * BLOCK
CN = 20
CBLK = 40
WIN = 5 * BLK
NB = WIN + CBLK
CHUNK = 256
NCH = ROWS // CHUNK
CPAD = 48
GRP = 4
LOG_CAP = 60.0
EARLY_X = ()
RELAY_AT = 0
LATE_X = (2, 3, 0, 1)
BF = jnp.bfloat16
F32 = jnp.float32
I32 = jnp.int32
MESH = pl.DeviceIdType.MESH
NT = (((1,), (1,)), ((), ()))
neg_large = -1e30


def rms(vals, gain):
    mean_square = jnp.mean(vals * vals, axis=-1, keepdims=True)
    return (vals * lax.rsqrt(mean_square + 1e-06) * gain).astype(BF)


def place(x, y, z, c):
    return (lax.rem(z, 2) * 4 + y, (z // 2) * 8 + x * 2 + c)


def gather_kernel(
    feats_hbm, gain_hbm, w_hbm, src_hbm, adj_hbm, fine_hbm, mask_hbm,
    qm, kv, lists, stats,
    feats, gain, w, src, adj, fine, mask, normed, nbr, picked, half, ag,
    send_n, recv_n, relay_send, a_sem, b_send, b_recv, c_send, c_recv, d_send, d_recv, e_send, e_recv,
    k_send, k_recv, f_send, f_recv, s_sem, mine_out, their, in_sem,
):
    r = lax.axis_index("region")
    s = lax.axis_index("sub")
    z_lo, y = r // 4, lax.rem(r, 4)
    z_hi, x, c = s // 8, lax.rem(s // 2, 4), lax.rem(s, 2)
    z = z_hi * 2 + z_lo
    zi = z_lo * 2 + z_hi
    me = r * 16 + s
    has = [r > 0, r < 7, jnp.where(c == 0, s > 0, s < 15)]
    partner = (r, s + 1 - 2 * c)
    y_next, y_prev = (place(x, lax.rem(y + k, 4), z, c) for k in (1, 3))
    z_next, z_prev, z_far = (place(x, y, lax.rem(z + k, 4), c) for k in (1, 3, 2))
    x_next, x_prev = (place(lax.rem(x + k, 4), y, z, c) for k in (1, 3))
    nbr_dev = [(r - 1, s), (r + 1, s), (r, s - 1 + 2 * c)]

    loads = [
        pltpu.make_async_copy(a, b, in_sem.at[i])
        for i, (a, b) in enumerate(
            ((src_hbm, src), (gain_hbm, gain), (feats_hbm, feats), (w_hbm, w), (adj_hbm, adj), (fine_hbm, fine), (mask_hbm, mask))
        )
    ]
    for load in loads:
        load.start()

    for d in range(3):

        @pl.when(jnp.logical_not(has[d]))
        def _():
            nbr[d] = jnp.zeros((ROWS, D), BF)

    barrier = pltpu.get_barrier_semaphore()
    for dev in (partner, y_next, y_prev, z_next, z_prev, z_far, x_next, x_prev):
        pl.semaphore_signal(barrier, inc=1, device_id=dev, device_id_type=MESH)
    for d in range(3):

        @pl.when(has[d])
        def _():
            pl.semaphore_signal(barrier, inc=1, device_id=nbr_dev[d], device_id_type=MESH)

    for load in loads[:3]:
        load.wait()
    src_row = (src[...] - me * ROWS).astype(F32)
    rows32 = lax.broadcasted_iota(I32, (32, CN), 0)
    cols32 = lax.broadcasted_iota(I32, (32, CN), 1)
    src_col = jnp.sum(jnp.where(rows32 == cols32, src_row, 0.0), axis=1, keepdims=True).astype(I32)
    hot = (lax.broadcasted_iota(I32, (32, ROWS), 1) == src_col).astype(BF)
    mine = rms(jnp.dot(hot, feats[...], preferred_element_type=F32), gain[...])
    picked[0] = mine[:, : D // 2]
    picked[1] = mine[:, D // 2 :]

    n_near = 8 + sum(h.astype(I32) for h in has)
    pl.semaphore_wait(barrier, n_near)

    def copy(src_ref, dst_ref, ss, rs, dev):
        return pltpu.make_async_remote_copy(
            src_ref=src_ref, dst_ref=dst_ref, send_sem=ss, recv_sem=rs, device_id=dev, device_id_type=MESH
        )

    a_copy = copy(picked.at[1 - c], half, a_sem.at[0], a_sem.at[1], partner)
    a_copy.start()

    def land(d):
        return d ^ 1 if d < 2 else 2

    def send_side(d, ch, dev, slot=None):
        slot = land(d) if slot is None else slot
        rows = pl.ds(pl.multiple_of(ch * CHUNK, CHUNK), CHUNK)
        return copy(normed.at[rows], nbr.at[slot, rows], send_n.at[d, ch], recv_n.at[slot, ch], dev)

    def relay_side(d, ch, dev):
        rows = pl.ds(pl.multiple_of(ch * CHUNK, CHUNK), CHUNK)
        return copy(nbr.at[d, rows], nbr.at[d ^ 1, rows], relay_send.at[ch - 2], recv_n.at[d ^ 1, ch], dev)

    def side_to(d, ch):
        if d >= 2:
            return nbr_dev[d], 2
        turn = ((r == 4) if d == 0 else (r == 3)) & (ch >= 2)
        far = 0 if d == 0 else 7
        return (jnp.where(turn, far, nbr_dev[d][0]), s), jnp.where(turn, d, d ^ 1)

    def start_sides(dirs, ch, crossing=None):
        for d in dirs:
            now = has[d]
            if crossing is not None:
                over = (r == 4) if d == 0 else (r == 3) if d == 1 else (r < 0)
                now = now & (over if crossing else jnp.logical_not(over))

            @pl.when(now)
            def _():
                send_side(d, ch, *side_to(d, ch)).start()

    def norm_chunk(ch):
        rows = pl.ds(ch * CHUNK, CHUNK)
        normed[rows] = rms(feats[rows].astype(F32), gain[...])

    norm_chunk(2)
    a_copy.wait()
    r48 = lax.broadcasted_iota(I32, (CPAD, 64), 0)
    c48 = lax.broadcasted_iota(I32, (CPAD, 64), 1)
    first = r48 < CN
    pick = jnp.where(first, r48, r48 + 12) == c48
    pick = (pick & (r48 < 2 * CN)).astype(BF)
    own_half = picked[c]
    lo = jnp.where(c == 0, own_half, half[...])
    hi = jnp.where(c == 0, half[...], own_half)
    block = jnp.dot(pick, jnp.concatenate([lo, hi], axis=0), preferred_element_type=F32).astype(BF)
    for p in range(2):
        ag[c, p, x, zi, y] = block[:, p * 128 : (p + 1) * 128]

    blk_ref = ag.at[c, :, x, zi, y]
    b_copies = [copy(blk_ref, blk_ref, b_send.at[i], b_recv.at[i], dev) for i, dev in enumerate((z_next, z_prev, z_far))]
    for b in b_copies:
        b.start()
    for ch in (3, 0, 1):
        norm_chunk(ch)
    for load in loads[3:]:
        load.wait()

    heads_of = (lax.broadcasted_iota(I32, (D, 128), 0) // HW == lax.broadcasted_iota(I32, (D, 128), 1)).astype(BF)
    stats[...] = jnp.zeros_like(stats)

    def top_norm(vals):
        sq = (vals.astype(F32) * vals.astype(F32)).astype(BF)
        sums = jnp.dot(sq, heads_of, preferred_element_type=F32)
        return jnp.max(sums, axis=0, keepdims=True)

    def put_kv(vals, block, count):
        kv[pl.ds(block, count)] = vals.reshape(count, BLOCK, 2 * D)
        stats[0:1] = jnp.maximum(stats[0:1], top_norm(vals[:, :D]))

    def k_copy(ch):
        there = pl.ds((3 + c) * BLK + 4 * ch, 4)
        return copy(kv.at[pl.ds(4 * ch, 4)], kv.at[there], k_send.at[ch], k_recv.at[ch], partner)

    lane_head = lax.broadcasted_iota(I32, (CHUNK, 256), 1) // HW

    def own_chunk(ch):
        vals = normed[pl.ds(ch * CHUNK, CHUNK)]
        qv = jnp.dot(vals, w[:, :D], preferred_element_type=F32).astype(BF) * jnp.asarray(HW**-0.5, BF)
        stats[1:2] = jnp.maximum(stats[1:2], top_norm(qv))
        for g in range(2):
            for h in range(4):
                qh = jnp.where(lane_head == h, qv[:, g * 256 : (g + 1) * 256], jnp.zeros((), BF))
                qm[pl.ds(4 * ch, 4), g, h * BLOCK : (h + 1) * BLOCK, :] = qh.reshape(4, BLOCK, 256)
        put_kv(jnp.dot(vals, w[:, D:], preferred_element_type=F32).astype(BF), 4 * ch, 4)
        k_copy(ch).start()

    for b in b_copies:
        b.wait()

    def side_part(ch, dirs, crossing=None):
        for d in dirs:
            over = (r == 4) if d == 0 else (r == 3) if d == 1 else (r < 0)

            def take():
                @pl.when(has[d])
                def _():
                    send_side(land(d), ch, nbr_dev[d]).wait_recv()

                rows = pl.ds(pl.multiple_of(ch * CHUNK, CHUNK), CHUNK)
                vals = jnp.dot(nbr[d, rows], w[:, D:], preferred_element_type=F32).astype(BF)
                put_kv(vals, ((d + 1) if d < 2 else (3 + c)) * BLK + 4 * ch, 4)

            if crossing is None:
                take()
            else:
                pl.when(over if crossing else jnp.logical_not(over))(take)

    def rings(kinds, early, late):
        sets = []
        for slab, at, nxt, prv, snd, rcv in kinds:
            prev_at, next_at = lax.rem(at + 3, 4), lax.rem(at + 1, 4)
            sets.append((
                [copy(slab(at, h), slab(at, h), snd.at[0, h], rcv.at[0, h], nxt) for h in range(2)],
                [copy(slab(at, h), slab(at, h), snd.at[1, h], rcv.at[1, h], prv) for h in range(2)],
                copy(slab(prev_at, 0), slab(prev_at, 0), snd.at[2, 0], rcv.at[2, 0], nxt),
                copy(slab(next_at, 1), slab(next_at, 1), snd.at[2, 1], rcv.at[2, 1], prv),
            ))
        for to_next, to_prev, _, _ in sets:
            to_next[0].start()
            to_prev[1].start()
        for to_next, to_prev, _, _ in sets:
            to_next[1].start()
            to_prev[0].start()
        early()
        for to_next, to_prev, on_next, on_prev in sets:
            to_next[0].wait_recv()
            on_next.start()
            to_prev[1].wait_recv()
            on_prev.start()
        for to_next, to_prev, _, _ in sets:
            to_next[1].wait_recv()
            to_prev[0].wait_recv()
        late()
        for to_next, to_prev, on_next, on_prev in sets:
            on_next.wait_recv()
            on_prev.wait_recv()
            for a in to_next + to_prev + [on_next, on_prev]:
                a.wait_send()

    def find_lists():
        dev_of, local = adj[...] // BLK, lax.rem(adj[...], BLK)
        gap = dev_of - me
        side = jnp.where(gap == -16, 1, jnp.where(gap == 16, 2, jnp.where(gap == -1, 3, jnp.where(gap == 1, 4, 0))))
        slot = side * BLK + local
        fine_live = (fine[...] == 1) | (lax.broadcasted_iota(I32, (NADJ, BLK), 0) == 0)
        fine_n = fine_live.astype(I32)
        eye = (lax.broadcasted_iota(I32, (BLK, BLK), 0) == lax.broadcasted_iota(I32, (BLK, BLK), 1)).astype(BF)
        coarse_n = lax.dot_general(
            (mask[...] == 1).astype(BF), eye, (((0,), (0,)), ((), ())), preferred_element_type=F32
        ).astype(I32)
        spot = lax.broadcasted_iota(I32, (56, BLK), 0)
        found = jnp.full((56, BLK), NB, I32)
        count = jnp.zeros((1, BLK), I32)
        for j in range(CBLK):
            live = coarse_n[j : j + 1]
            found = jnp.where(spot == jnp.where(live == 1, count, -1), WIN + j, found)
            count = count + live
        for j in range(NADJ):
            live = fine_n[j : j + 1]
            found = jnp.where(spot == jnp.where(live == 1, count, -1), slot[j : j + 1], found)
            count = count + live
        lists[...] = jnp.zeros_like(lists)
        lists[:, :BLK] = jnp.where(spot == 48, count, found)
        kv[NB] = jnp.zeros((BLOCK, 2 * D), BF)

    def c_early():
        for ch in (2, 3):
            start_sides((0, 1), ch, True)
        own_chunk(0)
        find_lists()

    rings(
        [
            (lambda i, h: ag.at[c, :, x, pl.ds(2 * h, 2), i], y, y_next, y_prev, c_send.at[0], c_recv.at[0]),
        ],
        c_early, lambda: None,
    )

    def e_copy(i):
        part = ag.at[c, :, i, pl.ds(2 * (1 - c), 2)]
        return copy(part, part, e_send.at[i], e_recv.at[i], partner)

    def e_start(i):
        e_copy(i).start()

    def d_early():
        e_start(x)
        for ch in (0, 1):
            start_sides((0, 1), ch, True)

        def sides(i, carry):
            start_sides((0, 1), lax.rem(i + 2, NCH), False)
            return carry

        lax.fori_loop(0, NCH, sides, 0)
        own_chunk(1)
        own_chunk(2)
        own_chunk(3)

    def pass_on():
        for at, d, to in ((7, 1, 4), (0, 0, 3)):

            @pl.when(r == at)
            def _():
                for ch in (2, 3):
                    send_side(d ^ 1, ch, (to, s)).wait_recv()
                    relay_side(d, ch, (to, s)).start()

    def d_late():
        e_start(lax.rem(x + 3, 4))
        e_start(lax.rem(x + 1, 4))
        for ch in LATE_X:
            start_sides((2,), ch)
        if RELAY_AT == 2:
            pass_on()

    rings(
        [
            (lambda i, h: ag.at[c, :, i, pl.ds(2 * h, 2)], x, x_next, x_prev, d_send.at[0], d_recv.at[0]),
        ],
        d_early, d_late,
    )
    e_start(lax.rem(x + 2, 4))
    if RELAY_AT == 0:
        pass_on()
    if RELAY_AT < 2:
        side_part(2, (0, 1), False)

    def e_wait(i, carry):
        e_copy(i).wait()
        return carry

    lax.fori_loop(0, 4, e_wait, 0)

    r160 = lax.broadcasted_iota(I32, (160, 4 * CPAD), 0)
    c160 = lax.broadcasted_iota(I32, (160, 4 * CPAD), 1)
    sel = ((r160 // 40) * CPAD + lax.rem(r160, 40) == c160).astype(BF)

    def f_copy(yy):
        part = kv.at[pl.ds(WIN + 5 * (4 * c + yy), 5)]
        return copy(part, part, f_send.at[yy], f_recv.at[yy], partner)

    def coarse_part(yy, carry):
        parts = []
        for zh in range(2):
            got = jnp.concatenate(
                [
                    jnp.concatenate([ag[h, p, k, 2 * c + zh, yy] for k in range(4)], axis=0)
                    for h in range(2)
                    for p in range(2)
                ],
                axis=1,
            )
            parts.append(jnp.dot(sel, got, preferred_element_type=F32).astype(BF))
        vals = jnp.concatenate(parts, axis=0)
        put_kv(jnp.dot(vals, w[:, D:], preferred_element_type=F32).astype(BF), WIN + 5 * (4 * c + yy), 5)
        f_copy(yy).start()
        return carry

    lax.fori_loop(0, 4, coarse_part, 0)
    if RELAY_AT == 1:
        pass_on()
    if RELAY_AT == 2:
        side_part(2, (0, 1), False)
    mine_out[...] = stats[...]
    s_copy = copy(mine_out, their, s_sem.at[0], s_sem.at[1], partner)
    s_copy.start()
    side_part(3, (0, 1), False)
    side_part(2, (2,))
    side_part(3, (2,))

    def rest(i, carry):
        side_part(i, (0, 1, 2))
        return carry

    lax.fori_loop(0, 2, rest, 0)

    def crossed(i, carry):
        side_part(i + 2, (0, 1), True)
        return carry

    lax.fori_loop(0, 2, crossed, 0)
    s_copy.wait()
    stats[...] = jnp.maximum(stats[...], their[...])

    def send_wait(ch, carry):
        k_copy(ch).wait()
        f_copy(ch).wait()
        for d in range(3):

            @pl.when(has[d])
            def _():
                send_side(d, ch, nbr_dev[d]).wait_send()

        return carry

    lax.fori_loop(0, NCH, send_wait, 0)
    for at, d, to in ((7, 1, 4), (0, 0, 3)):

        @pl.when(r == at)
        def _():
            for ch in (2, 3):
                relay_side(d, ch, (to, s)).wait_send()


def attend_kernel(unroll, lists_vmem, qm, kv, stats, gain_hbm, w_hbm, out, lists, gain, w, mid, acc, lsum, sems):
    loads = [
        pltpu.make_async_copy(a, b, sems.at[i])
        for i, (a, b) in enumerate(((lists_vmem, lists), (gain_hbm, gain), (w_hbm, w)))
    ]
    for load in loads:
        load.start()
    lane = lax.broadcasted_iota(I32, (BLOCK, 256), 1) // HW
    acc[...] = jnp.zeros_like(acc)
    lsum[...] = jnp.zeros_like(lsum)
    for load in loads:
        load.wait()

    bound = jnp.max(jnp.sqrt(stats[0:1]) * jnp.sqrt(stats[1:2])) * 1.02
    safe = bound < LOG_CAP

    def groups(b):
        return jnp.where(b < BLK, (lists[48, jnp.minimum(b, BLK - 1)] + GRP - 1) // GRP, 0)

    def blocks_of(b, t, lo):
        bb = jnp.minimum(b, BLK - 1)
        return jnp.concatenate([kv[lists[t * GRP + j, bb], :, lo : lo + 256] for j in range(GRP)], axis=0)

    def scores(b, t, g):
        return lax.dot_general(qm[jnp.minimum(b, BLK - 1), g], blocks_of(b, t, g * 256), NT, preferred_element_type=F32)

    key_lane = lax.broadcasted_iota(I32, (1, 256), 1)

    def open_keys(b, t):
        bb = jnp.minimum(b, BLK - 1)
        return key_lane < (lists[48, bb] - t * GRP) * BLOCK

    def add_up(b, t, g, p, keys):
        kept = jnp.where(keys, p, 0.0)
        lsum[b, g] += kept[:, :128] + kept[:, 128:]
        acc[b, g] += jnp.dot(p.astype(BF), blocks_of(b, t, D + g * 256), preferred_element_type=F32)

    @pl.when(safe)
    def _():
        total = functools.reduce(lambda a, b: a + b, [groups(b) for b in range(BLK)])

        def step_on(b, t):
            last = t + 1 >= groups(b)
            return jnp.where(last, jnp.minimum(b + 1, BLK), b), jnp.where(last, 0, t + 1)

        def body(i, at):
            spots = [at]
            for _ in range(unroll):
                spots.append(step_on(*spots[-1]))
            held = [scores(*spots[0], g) for g in range(2)]
            for u in range(unroll):
                later = [scores(*spots[u + 1], g) for g in range(2)] if u + 1 < unroll else None
                keys = open_keys(*spots[u])
                for g in range(2):
                    add_up(*spots[u], g, jnp.exp(held[g]), keys)
                held = later
            return spots[-1]

        lax.fori_loop(0, (total + unroll - 1) // unroll, body, (jnp.int32(0), jnp.int32(0)))

    @pl.when(jnp.logical_not(safe))
    def _():
        def block(b, carry):
            for g in range(2):
                def peak(t, m):
                    sc = jnp.where(open_keys(b, t), scores(b, t, g), neg_large)
                    return jnp.maximum(m, jnp.max(sc, axis=-1, keepdims=True))

                top = lax.fori_loop(0, groups(b), peak, jnp.full((256, 1), neg_large, F32))

                def weigh(t, carry):
                    keys = open_keys(b, t)
                    sc = jnp.where(keys, scores(b, t, g), neg_large)
                    add_up(b, t, g, jnp.exp(sc - top), keys)
                    return carry

                lax.fori_loop(0, groups(b), weigh, 0)
            return carry

        lax.fori_loop(0, BLK, block, 0)

    def finish(i, carry):
        for k in range(4):
            b = 4 * i + k
            pieces = []
            for g in range(2):
                piece = jnp.zeros((BLOCK, 256), F32)
                for h in range(4):
                    rows = slice(h * BLOCK, (h + 1) * BLOCK)
                    total = jnp.sum(lsum[b, g, rows, :], axis=-1, keepdims=True)
                    piece = jnp.where(lane == h, acc[b, g, rows, :] / total, piece)
                pieces.append(piece)
            attended = jnp.concatenate(pieces, axis=1).astype(BF).astype(F32)
            mid[k * BLOCK : (k + 1) * BLOCK] = rms(attended, gain[...])
        rows = pl.ds(pl.multiple_of(i * CHUNK, CHUNK), CHUNK)
        out[rows] = jnp.dot(mid[...], w[...], preferred_element_type=F32).astype(BF)
        return carry

    lax.fori_loop(0, 4, finish, 0)


def per_device(node_feats, gain_in, w_qkv, gain_out, w_out, adjacency, fine_valid, coarse_mask, coarse_src):
    vmem = pl.BlockSpec(memory_space=pltpu.VMEM)
    hbm = pl.BlockSpec(memory_space=pltpu.HBM)
    dma = pltpu.SemaphoreType.DMA
    qm, kv, lists, stats = pl.pallas_call(
        gather_kernel,
        out_shape=(
            jax.ShapeDtypeStruct((BLK, 2, 256, 256), BF),
            jax.ShapeDtypeStruct((NB + 1, BLOCK, 2 * D), BF),
            jax.ShapeDtypeStruct((56, 128), I32),
            jax.ShapeDtypeStruct((8, 128), F32),
        ),
        in_specs=[hbm] * 7,
        out_specs=(vmem,) * 4,
        scratch_shapes=[
            pltpu.VMEM((ROWS, D), BF),
            pltpu.VMEM((1, D), F32),
            pltpu.VMEM((D, 3 * D), BF),
            pltpu.VMEM((1, CN), I32),
            pltpu.VMEM((NADJ, BLK), I32),
            pltpu.VMEM((NADJ, BLK), I32),
            pltpu.VMEM((BLK, CBLK), I32),
            pltpu.VMEM((ROWS, D), BF),
            pltpu.VMEM((3, ROWS, D), BF),
            pltpu.VMEM((2, 32, D // 2), BF),
            pltpu.VMEM((32, D // 2), BF),
            pltpu.VMEM((2, 2, 4, 4, 4, CPAD, D // 4), BF),
            dma((3, 4)), dma((3, 4)), dma((2,)), dma((2,)), dma((3,)), dma((3,)),
            dma((1, 3, 2)), dma((1, 3, 2)), dma((1, 3, 2)), dma((1, 3, 2)), dma((4,)), dma((4,)),
            dma((4,)), dma((4,)), dma((4,)), dma((4,)), dma((2,)),
            pltpu.VMEM((8, 128), F32), pltpu.VMEM((8, 128), F32),
            dma((7,)),
        ],
        compiler_params=pltpu.CompilerParams(
            collective_id=0, has_side_effects=True, vmem_limit_bytes=24 * 2**20
        ),
    )(
        *(
            pltpu.with_memory_space_constraint(a, pltpu.HBM)
            for a in (
                node_feats, gain_in.reshape(1, D), w_qkv, coarse_src.reshape(1, CN),
                adjacency.T, fine_valid.T, coarse_mask,
            )
        )
    )
    return pl.pallas_call(
        functools.partial(attend_kernel, 8),
        out_shape=jax.ShapeDtypeStruct((ROWS, D), BF),
        in_specs=[vmem, vmem, vmem, vmem, hbm, hbm],
        out_specs=vmem,
        scratch_shapes=[
            pltpu.SMEM((56, 128), I32),
            pltpu.VMEM((1, D), F32),
            pltpu.VMEM((D, D), BF),
            pltpu.VMEM((CHUNK, D), BF),
            pltpu.VMEM((BLK + 1, 2, 256, 256), F32),
            pltpu.VMEM((BLK + 1, 2, 256, 128), F32),
            dma((3,)),
        ],
        compiler_params=pltpu.CompilerParams(vmem_limit_bytes=28 * 2**20),
    )(lists, qm, kv, stats, *(
        pltpu.with_memory_space_constraint(a, pltpu.HBM) for a in (gain_out.reshape(1, D), w_out)
    ))


def solution(mesh):
    both = ("region", "sub")
    in_specs = (P(both, None), P(), P(), P(), P(), P(both, None), P(both, None), P(both, None), P(both))
    return jax.shard_map(per_device, mesh=mesh, in_specs=in_specs, out_specs=P(both, None), check_vma=False)
```

```python
import functools

import jax
import jax.numpy as jnp
from jax import lax
from jax.experimental import pallas as pl
from jax.experimental.pallas import tpu as pltpu
from jax.sharding import PartitionSpec as P

D = 512
HEADS = 8
HW = D // HEADS
BLOCK = 64
NADJ = 7
BLK = 16
ROWS = BLK * BLOCK
CN = 20
CBLK = 40
WIN = 5 * BLK
NB = WIN + CBLK
CHUNK = 256
NCH = ROWS // CHUNK
CPAD = 48
GRP = 4
UNROLL = 8
LOG_CAP = 60.0
BF = jnp.bfloat16
F32 = jnp.float32
I32 = jnp.int32
MESH = pl.DeviceIdType.MESH
NT = (((1,), (1,)), ((), ()))
neg_large = -1e30


def rms(vals, gain):
    mean_square = jnp.mean(vals * vals, axis=-1, keepdims=True)
    return (vals * lax.rsqrt(mean_square + 1e-06) * gain).astype(BF)


def place(x, y, z, c):
    return (lax.rem(z, 2) * 4 + y, (z // 2) * 8 + x * 2 + c)


def gather_kernel(
    feats_hbm, gain_hbm, w_hbm, src_hbm, adj_hbm, fine_hbm, mask_hbm,
    qm, kv, lists, stats,
    feats, gain, w, src, adj, fine, mask, normed, nbr, picked, half, along_z, ag,
    send_n, recv_n, relay_send, a_sem, b_send, b_recv, c_send, c_recv, d_send, d_recv, e_send, e_recv,
    k_send, k_recv, f_send, f_recv, s_sem, mine_out, their, in_sem,
):
    r = lax.axis_index("region")
    s = lax.axis_index("sub")
    z_lo, y = r // 4, lax.rem(r, 4)
    z_hi, x, c = s // 8, lax.rem(s // 2, 4), lax.rem(s, 2)
    z = z_hi * 2 + z_lo
    zi = z_lo * 2 + z_hi
    me = r * 16 + s
    has = [r > 0, r < 7, jnp.where(c == 0, s > 0, s < 15)]
    partner = (r, s + 1 - 2 * c)
    y_next, y_prev = (place(x, lax.rem(y + k, 4), z, c) for k in (1, 3))
    z_next, z_prev, z_far = (place(x, y, lax.rem(z + k, 4), c) for k in (1, 3, 2))
    x_next, x_prev = (place(lax.rem(x + k, 4), y, z, c) for k in (1, 3))
    nbr_dev = [(r - 1, s), (r + 1, s), (r, s - 1 + 2 * c)]

    loads = [
        pltpu.make_async_copy(a, b, in_sem.at[i])
        for i, (a, b) in enumerate(
            ((src_hbm, src), (gain_hbm, gain), (feats_hbm, feats), (w_hbm, w), (adj_hbm, adj), (fine_hbm, fine), (mask_hbm, mask))
        )
    ]
    for load in loads:
        load.start()

    for d in range(3):

        @pl.when(jnp.logical_not(has[d]))
        def _():
            nbr[d] = jnp.zeros((ROWS, D), BF)

    barrier = pltpu.get_barrier_semaphore()
    for dev in (partner, y_next, y_prev, z_next, z_prev, z_far, x_next, x_prev):
        pl.semaphore_signal(barrier, inc=1, device_id=dev, device_id_type=MESH)
    for d in range(3):

        @pl.when(has[d])
        def _():
            pl.semaphore_signal(barrier, inc=1, device_id=nbr_dev[d], device_id_type=MESH)

    for load in loads[:3]:
        load.wait()
    src_row = (src[...] - me * ROWS).astype(F32)
    rows32 = lax.broadcasted_iota(I32, (32, CN), 0)
    cols32 = lax.broadcasted_iota(I32, (32, CN), 1)
    src_col = jnp.sum(jnp.where(rows32 == cols32, src_row, 0.0), axis=1, keepdims=True).astype(I32)
    hot = (lax.broadcasted_iota(I32, (32, ROWS), 1) == src_col).astype(BF)
    mine = rms(jnp.dot(hot, feats[...], preferred_element_type=F32), gain[...])
    picked[0] = mine[:, : D // 2]
    picked[1] = mine[:, D // 2 :]

    n_near = 8 + sum(h.astype(I32) for h in has)
    pl.semaphore_wait(barrier, n_near)

    def copy(src_ref, dst_ref, ss, rs, dev):
        return pltpu.make_async_remote_copy(
            src_ref=src_ref, dst_ref=dst_ref, send_sem=ss, recv_sem=rs, device_id=dev, device_id_type=MESH
        )

    a_copy = copy(picked.at[1 - c], half, a_sem.at[0], a_sem.at[1], partner)
    a_copy.start()

    def land(d):
        return d ^ 1 if d < 2 else 2

    def send_side(d, ch, dev, slot=None):
        slot = land(d) if slot is None else slot
        rows = pl.ds(pl.multiple_of(ch * CHUNK, CHUNK), CHUNK)
        return copy(normed.at[rows], nbr.at[slot, rows], send_n.at[d, ch], recv_n.at[slot, ch], dev)

    def relay_side(d, ch, dev):
        rows = pl.ds(pl.multiple_of(ch * CHUNK, CHUNK), CHUNK)
        return copy(nbr.at[d, rows], nbr.at[d ^ 1, rows], relay_send.at[ch - 2], recv_n.at[d ^ 1, ch], dev)

    def side_to(d, ch):
        if d >= 2:
            return nbr_dev[d], 2
        turn = ((r == 4) if d == 0 else (r == 3)) & (ch >= 2)
        far = 0 if d == 0 else 7
        return (jnp.where(turn, far, nbr_dev[d][0]), s), jnp.where(turn, d, d ^ 1)

    def start_sides(dirs, ch, crossing=None):
        for d in dirs:
            now = has[d]
            if crossing is not None:
                over = (r == 4) if d == 0 else (r == 3) if d == 1 else (r < 0)
                now = now & (over if crossing else jnp.logical_not(over))

            @pl.when(now)
            def _():
                send_side(d, ch, *side_to(d, ch)).start()

    def norm_chunk(ch):
        rows = pl.ds(ch * CHUNK, CHUNK)
        normed[rows] = rms(feats[rows].astype(F32), gain[...])

    norm_chunk(2)
    a_copy.wait()
    r48 = lax.broadcasted_iota(I32, (CPAD, 64), 0)
    c48 = lax.broadcasted_iota(I32, (CPAD, 64), 1)
    first = r48 < CN
    pick = jnp.where(first, r48, r48 + 12) == c48
    pick = (pick & (r48 < 2 * CN)).astype(BF)
    own_half = picked[c]
    lo = jnp.where(c == 0, own_half, half[...])
    hi = jnp.where(c == 0, half[...], own_half)
    block = jnp.dot(pick, jnp.concatenate([lo, hi], axis=0), preferred_element_type=F32).astype(BF)
    along_z[zi] = block

    blk_ref = along_z.at[zi]
    b_copies = [copy(blk_ref, blk_ref, b_send.at[i], b_recv.at[i], dev) for i, dev in enumerate((z_next, z_prev, z_far))]
    for b in b_copies:
        b.start()
    for ch in (3, 0, 1):
        norm_chunk(ch)
    for load in loads[3:]:
        load.wait()

    heads_of = (lax.broadcasted_iota(I32, (D, 128), 0) // HW == lax.broadcasted_iota(I32, (D, 128), 1)).astype(BF)
    stats[...] = jnp.zeros_like(stats)

    def top_norm(vals):
        sq = (vals.astype(F32) * vals.astype(F32)).astype(BF)
        sums = jnp.dot(sq, heads_of, preferred_element_type=F32)
        return jnp.max(sums, axis=0, keepdims=True)

    def put_kv(vals, block, count):
        kv[pl.ds(block, count)] = vals.reshape(count, BLOCK, 2 * D)
        stats[0:1] = jnp.maximum(stats[0:1], top_norm(vals[:, :D]))

    def k_copy(ch):
        there = pl.ds((3 + c) * BLK + 4 * ch, 4)
        return copy(kv.at[pl.ds(4 * ch, 4)], kv.at[there], k_send.at[ch], k_recv.at[ch], partner)

    lane_head = lax.broadcasted_iota(I32, (CHUNK, 256), 1) // HW

    def own_chunk(ch):
        vals = normed[pl.ds(ch * CHUNK, CHUNK)]
        qv = jnp.dot(vals, w[:, :D], preferred_element_type=F32).astype(BF) * jnp.asarray(HW**-0.5, BF)
        stats[1:2] = jnp.maximum(stats[1:2], top_norm(qv))
        for g in range(2):
            for h in range(4):
                qh = jnp.where(lane_head == h, qv[:, g * 256 : (g + 1) * 256], jnp.zeros((), BF))
                qm[pl.ds(4 * ch, 4), g, h * BLOCK : (h + 1) * BLOCK, :] = qh.reshape(4, BLOCK, 256)
        put_kv(jnp.dot(vals, w[:, D:], preferred_element_type=F32).astype(BF), 4 * ch, 4)
        k_copy(ch).start()

    for b in b_copies:
        b.wait()
    r80 = lax.broadcasted_iota(I32, (80, 2 * CPAD), 0)
    c80 = lax.broadcasted_iota(I32, (80, 2 * CPAD), 1)
    tight = ((r80 // 40) * CPAD + lax.rem(r80, 40) == c80).astype(BF)
    for h in range(2):
        both = jnp.concatenate([along_z[2 * h], along_z[2 * h + 1]], axis=0)
        ag[c, x, h, y] = jnp.dot(tight, both, preferred_element_type=F32).astype(BF)

    def side_part(ch, dirs, crossing=None):
        for d in dirs:
            over = (r == 4) if d == 0 else (r == 3) if d == 1 else (r < 0)

            def take():
                @pl.when(has[d])
                def _():
                    send_side(land(d), ch, nbr_dev[d]).wait_recv()

                rows = pl.ds(pl.multiple_of(ch * CHUNK, CHUNK), CHUNK)
                vals = jnp.dot(nbr[d, rows], w[:, D:], preferred_element_type=F32).astype(BF)
                put_kv(vals, ((d + 1) if d < 2 else (3 + c)) * BLK + 4 * ch, 4)

            if crossing is None:
                take()
            else:
                pl.when(over if crossing else jnp.logical_not(over))(take)

    def rings(kinds, early, late):
        sets = []
        for slab, at, nxt, prv, snd, rcv in kinds:
            prev_at, next_at = lax.rem(at + 3, 4), lax.rem(at + 1, 4)
            sets.append((
                [copy(slab(at, h), slab(at, h), snd.at[0, h], rcv.at[0, h], nxt) for h in range(2)],
                [copy(slab(at, h), slab(at, h), snd.at[1, h], rcv.at[1, h], prv) for h in range(2)],
                copy(slab(prev_at, 0), slab(prev_at, 0), snd.at[2, 0], rcv.at[2, 0], nxt),
                copy(slab(next_at, 1), slab(next_at, 1), snd.at[2, 1], rcv.at[2, 1], prv),
            ))
        for to_next, to_prev, _, _ in sets:
            to_next[0].start()
            to_prev[1].start()
        for to_next, to_prev, _, _ in sets:
            to_next[1].start()
            to_prev[0].start()
        early()
        for to_next, to_prev, on_next, on_prev in sets:
            to_next[0].wait_recv()
            on_next.start()
            to_prev[1].wait_recv()
            on_prev.start()
        for to_next, to_prev, _, _ in sets:
            to_next[1].wait_recv()
            to_prev[0].wait_recv()
        late()
        for to_next, to_prev, on_next, on_prev in sets:
            on_next.wait_recv()
            on_prev.wait_recv()
            for a in to_next + to_prev + [on_next, on_prev]:
                a.wait_send()

    def find_lists():
        dev_of, local = adj[...] // BLK, lax.rem(adj[...], BLK)
        gap = dev_of - me
        side = jnp.where(gap == -16, 1, jnp.where(gap == 16, 2, jnp.where(gap == -1, 3, jnp.where(gap == 1, 4, 0))))
        slot = side * BLK + local
        fine_live = (fine[...] == 1) | (lax.broadcasted_iota(I32, (NADJ, BLK), 0) == 0)
        fine_n = fine_live.astype(I32)
        eye = (lax.broadcasted_iota(I32, (BLK, BLK), 0) == lax.broadcasted_iota(I32, (BLK, BLK), 1)).astype(BF)
        coarse_n = lax.dot_general(
            (mask[...] == 1).astype(BF), eye, (((0,), (0,)), ((), ())), preferred_element_type=F32
        ).astype(I32)
        spot = lax.broadcasted_iota(I32, (56, BLK), 0)
        found = jnp.full((56, BLK), NB, I32)
        count = jnp.zeros((1, BLK), I32)
        for j in range(CBLK):
            live = coarse_n[j : j + 1]
            found = jnp.where(spot == jnp.where(live == 1, count, -1), WIN + j, found)
            count = count + live
        for j in range(NADJ):
            live = fine_n[j : j + 1]
            found = jnp.where(spot == jnp.where(live == 1, count, -1), slot[j : j + 1], found)
            count = count + live
        lists[...] = jnp.zeros_like(lists)
        lists[:, :BLK] = jnp.where(spot == 48, count, found)
        kv[NB] = jnp.zeros((BLOCK, 2 * D), BF)

    def c_early():
        for ch in (2, 3):
            start_sides((0, 1), ch, True)
        own_chunk(0)
        find_lists()

    rings(
        [
            (lambda i, h: ag.at[c, x, h, i], y, y_next, y_prev, c_send.at[0], c_recv.at[0]),
        ],
        c_early, lambda: None,
    )

    def e_copy(i):
        part = ag.at[c, i, 1 - c]
        return copy(part, part, e_send.at[i], e_recv.at[i], partner)

    def e_start(i):
        e_copy(i).start()

    def d_early():
        e_start(x)
        for ch in (0, 1):
            start_sides((0, 1), ch, True)

        def sides(i, carry):
            start_sides((0, 1), lax.rem(i + 2, NCH), False)
            return carry

        lax.fori_loop(0, NCH, sides, 0)
        own_chunk(1)
        own_chunk(2)
        own_chunk(3)

    def pass_on():
        for at, d, to in ((7, 1, 4), (0, 0, 3)):

            @pl.when(r == at)
            def _():
                for ch in (2, 3):
                    send_side(d ^ 1, ch, (to, s)).wait_recv()
                    relay_side(d, ch, (to, s)).start()

    def d_late():
        e_start(lax.rem(x + 3, 4))
        e_start(lax.rem(x + 1, 4))
        for ch in (2, 3, 0, 1):
            start_sides((2,), ch)

    rings(
        [
            (lambda i, h: ag.at[c, i, h], x, x_next, x_prev, d_send.at[0], d_recv.at[0]),
        ],
        d_early, d_late,
    )
    e_start(lax.rem(x + 2, 4))
    pass_on()
    side_part(2, (0, 1), False)

    def e_wait(i, carry):
        e_copy(i).wait()
        return carry

    lax.fori_loop(0, 4, e_wait, 0)

    def f_copy(yy):
        part = kv.at[pl.ds(WIN + 5 * (4 * c + yy), 5)]
        return copy(part, part, f_send.at[yy], f_recv.at[yy], partner)

    def coarse_part(yy, carry):
        cols = []
        for h in range(2):
            got = [ag[h, k, c, yy] for k in range(4)]
            cols.append(jnp.concatenate([g[40 * zh : 40 * zh + 40] for zh in range(2) for g in got], axis=0))
        vals = jnp.concatenate(cols, axis=1)
        put_kv(jnp.dot(vals, w[:, D:], preferred_element_type=F32).astype(BF), WIN + 5 * (4 * c + yy), 5)
        f_copy(yy).start()
        return carry

    lax.fori_loop(0, 4, coarse_part, 0)
    mine_out[...] = stats[...]
    s_copy = copy(mine_out, their, s_sem.at[0], s_sem.at[1], partner)
    s_copy.start()
    side_part(3, (0, 1), False)
    side_part(2, (2,))
    side_part(3, (2,))

    def rest(i, carry):
        side_part(i, (0, 1, 2))
        return carry

    lax.fori_loop(0, 2, rest, 0)

    def crossed(i, carry):
        side_part(i + 2, (0, 1), True)
        return carry

    lax.fori_loop(0, 2, crossed, 0)
    s_copy.wait()
    stats[...] = jnp.maximum(stats[...], their[...])

    def send_wait(ch, carry):
        k_copy(ch).wait()
        f_copy(ch).wait()
        for d in range(3):

            @pl.when(has[d])
            def _():
                send_side(d, ch, nbr_dev[d]).wait_send()

        return carry

    lax.fori_loop(0, NCH, send_wait, 0)
    for at, d, to in ((7, 1, 4), (0, 0, 3)):

        @pl.when(r == at)
        def _():
            for ch in (2, 3):
                relay_side(d, ch, (to, s)).wait_send()


def attend_kernel(unroll, lists_vmem, qm, kv, stats, gain_hbm, w_hbm, out, lists, gain, w, acc, lsum, sems):
    loads = [
        pltpu.make_async_copy(a, b, sems.at[i])
        for i, (a, b) in enumerate(((lists_vmem, lists), (gain_hbm, gain), (w_hbm, w)))
    ]
    for load in loads:
        load.start()
    lane = lax.broadcasted_iota(I32, (BLOCK, 256), 1) // HW
    acc[...] = jnp.zeros_like(acc)
    lsum[...] = jnp.zeros_like(lsum)
    for load in loads:
        load.wait()

    bound = jnp.max(jnp.sqrt(stats[0:1]) * jnp.sqrt(stats[1:2])) * 1.02
    safe = bound < LOG_CAP

    def groups(b):
        return jnp.where(b < BLK, (lists[48, jnp.minimum(b, BLK - 1)] + GRP - 1) // GRP, 0)

    def blocks_of(b, t, lo):
        bb = jnp.minimum(b, BLK - 1)
        return jnp.concatenate([kv[lists[t * GRP + j, bb], :, lo : lo + 256] for j in range(GRP)], axis=0)

    def scores(b, t, g):
        return lax.dot_general(qm[jnp.minimum(b, BLK - 1), g], blocks_of(b, t, g * 256), NT, preferred_element_type=F32)

    key_lane = lax.broadcasted_iota(I32, (1, GRP * BLOCK), 1)

    def open_keys(b, t):
        bb = jnp.minimum(b, BLK - 1)
        return key_lane < (lists[48, bb] - t * GRP) * BLOCK

    def count_up(b, g, p, keys):
        kept = jnp.where(keys, p, 0.0)
        lsum[b, g] += functools.reduce(
            lambda a, e: a + e, [kept[:, i : i + 128] for i in range(0, GRP * BLOCK, 128)]
        )
        return p.astype(BF)

    def mix(b, t, g, p):
        acc[b, g] += jnp.dot(p, blocks_of(b, t, D + g * 256), preferred_element_type=F32)

    def add_up(b, t, g, p, keys):
        mix(b, t, g, count_up(b, g, p, keys))

    @pl.when(safe)
    def _():
        total = functools.reduce(lambda a, b: a + b, [groups(b) for b in range(BLK)])

        def step_on(b, t):
            last = t + 1 >= groups(b)
            return jnp.where(last, jnp.minimum(b + 1, BLK), b), jnp.where(last, 0, t + 1)

        def body(i, at):
            spots = [at]
            for _ in range(unroll):
                spots.append(step_on(*spots[-1]))
            steps = [(u, g) for u in range(unroll) for g in range(2)]
            held = scores(*spots[0], 0)
            for k, (u, g) in enumerate(steps):
                later = None
                if k + 1 < len(steps):
                    nu, ng = steps[k + 1]
                    later = scores(*spots[nu], ng)
                add_up(*spots[u], g, jnp.exp(held), open_keys(*spots[u]))
                held = later
            return spots[-1]

        lax.fori_loop(0, (total + unroll - 1) // unroll, body, (jnp.int32(0), jnp.int32(0)))

    @pl.when(jnp.logical_not(safe))
    def _():
        def block(b, carry):
            for g in range(2):
                def peak(t, m):
                    sc = jnp.where(open_keys(b, t), scores(b, t, g), neg_large)
                    return jnp.maximum(m, jnp.max(sc, axis=-1, keepdims=True))

                top = lax.fori_loop(0, groups(b), peak, jnp.full((256, 1), neg_large, F32))

                def weigh(t, carry):
                    keys = open_keys(b, t)
                    sc = jnp.where(keys, scores(b, t, g), neg_large)
                    add_up(b, t, g, jnp.exp(sc - top), keys)
                    return carry

                lax.fori_loop(0, groups(b), weigh, 0)
            return carry

        lax.fori_loop(0, BLK, block, 0)

    def finish(i):
        attended = []
        for b in range(4 * i, 4 * i + 4):
            pieces = []
            for g in range(2):
                piece = acc[b, g, :BLOCK, :]
                total = jnp.sum(lsum[b, g, :BLOCK, :], axis=-1, keepdims=True)
                for h in range(1, 4):
                    rows = slice(h * BLOCK, (h + 1) * BLOCK)
                    piece = jnp.where(lane == h, acc[b, g, rows, :], piece)
                    total = jnp.where(lane == h, jnp.sum(lsum[b, g, rows, :], axis=-1, keepdims=True), total)
                pieces.append(piece / total)
            row = jnp.concatenate(pieces, axis=1).astype(BF).astype(F32)
            attended.append(rms(row, gain[...]))
        rows = slice(i * CHUNK, (i + 1) * CHUNK)
        out[rows] = jnp.dot(jnp.concatenate(attended, axis=0), w[...], preferred_element_type=F32).astype(BF)

    for i in range(4):
        finish(i)


def attend_call(lists, qm, kv, stats, gain_out, w_out):
    vmem = pl.BlockSpec(memory_space=pltpu.VMEM)
    hbm = pl.BlockSpec(memory_space=pltpu.HBM)
    dma = pltpu.SemaphoreType.DMA
    return pl.pallas_call(
        functools.partial(attend_kernel, UNROLL),
        out_shape=jax.ShapeDtypeStruct((ROWS, D), BF),
        in_specs=[vmem, vmem, vmem, vmem, hbm, hbm],
        out_specs=vmem,
        scratch_shapes=[
            pltpu.SMEM((56, 128), I32),
            pltpu.VMEM((1, D), F32),
            pltpu.VMEM((D, D), BF),
            pltpu.VMEM((BLK + 1, 2, 256, 256), F32),
            pltpu.VMEM((BLK + 1, 2, 256, 128), F32),
            dma((3,)),
        ],
        compiler_params=pltpu.CompilerParams(vmem_limit_bytes=28 * 2**20),
    )(lists, qm, kv, stats, gain_out, w_out)


def per_device(node_feats, gain_in, w_qkv, gain_out, w_out, adjacency, fine_valid, coarse_mask, coarse_src):
    vmem = pl.BlockSpec(memory_space=pltpu.VMEM)
    hbm = pl.BlockSpec(memory_space=pltpu.HBM)
    dma = pltpu.SemaphoreType.DMA
    qm, kv, lists, stats = pl.pallas_call(
        gather_kernel,
        out_shape=(
            jax.ShapeDtypeStruct((BLK, 2, 256, 256), BF),
            jax.ShapeDtypeStruct((NB + 1, BLOCK, 2 * D), BF),
            jax.ShapeDtypeStruct((56, 128), I32),
            jax.ShapeDtypeStruct((8, 128), F32),
        ),
        in_specs=[hbm] * 7,
        out_specs=(vmem,) * 4,
        scratch_shapes=[
            pltpu.VMEM((ROWS, D), BF),
            pltpu.VMEM((1, D), F32),
            pltpu.VMEM((D, 3 * D), BF),
            pltpu.VMEM((1, CN), I32),
            pltpu.VMEM((NADJ, BLK), I32),
            pltpu.VMEM((NADJ, BLK), I32),
            pltpu.VMEM((BLK, CBLK), I32),
            pltpu.VMEM((ROWS, D), BF),
            pltpu.VMEM((3, ROWS, D), BF),
            pltpu.VMEM((2, 32, D // 2), BF),
            pltpu.VMEM((32, D // 2), BF),
            pltpu.VMEM((4, CPAD, D // 2), BF),
            pltpu.VMEM((2, 4, 2, 4, 80, D // 2), BF),
            dma((3, 4)), dma((3, 4)), dma((2,)), dma((2,)), dma((3,)), dma((3,)),
            dma((1, 3, 2)), dma((1, 3, 2)), dma((1, 3, 2)), dma((1, 3, 2)), dma((4,)), dma((4,)),
            dma((4,)), dma((4,)), dma((4,)), dma((4,)), dma((2,)),
            pltpu.VMEM((8, 128), F32), pltpu.VMEM((8, 128), F32),
            dma((7,)),
        ],
        compiler_params=pltpu.CompilerParams(
            collective_id=0, has_side_effects=True, vmem_limit_bytes=24 * 2**20
        ),
    )(
        *(
            pltpu.with_memory_space_constraint(a, pltpu.HBM)
            for a in (
                node_feats, gain_in.reshape(1, D), w_qkv, coarse_src.reshape(1, CN),
                adjacency.T, fine_valid.T, coarse_mask,
            )
        )
    )
    return attend_call(
        lists, qm, kv, stats,
        *(pltpu.with_memory_space_constraint(a, pltpu.HBM) for a in (gain_out.reshape(1, D), w_out)),
    )


def solution(mesh):
    both = ("region", "sub")
    in_specs = (P(both, None), P(), P(), P(), P(), P(both, None), P(both, None), P(both, None), P(both))
    return jax.shard_map(per_device, mesh=mesh, in_specs=in_specs, out_specs=P(both, None), check_vma=False)
```

```python
import functools

import jax
import jax.numpy as jnp
from jax import lax
from jax.experimental import pallas as pl
from jax.experimental.pallas import tpu as pltpu
from jax.sharding import PartitionSpec as P

D = 512
HEADS = 8
HW = D // HEADS
BLOCK = 64
NADJ = 7
BLK = 16
ROWS = BLK * BLOCK
CN = 20
CBLK = 40
WIN = 5 * BLK
NB = WIN + CBLK
CHUNK = 256
NCH = ROWS // CHUNK
CPAD = 48
GRP = 4
UNROLL = 10
LOG_CAP = 60.0
BF = jnp.bfloat16
F32 = jnp.float32
I32 = jnp.int32
MESH = pl.DeviceIdType.MESH
NT = (((1,), (1,)), ((), ()))
neg_large = -1e30


def rms(vals, gain):
    mean_square = jnp.mean(vals * vals, axis=-1, keepdims=True)
    return (vals * lax.rsqrt(mean_square + 1e-06) * gain).astype(BF)


def place(x, y, z, c):
    return (lax.rem(z, 2) * 4 + y, (z // 2) * 8 + x * 2 + c)


def gather_kernel(
    feats_hbm, gain_hbm, w_hbm, src_hbm, adj_hbm, fine_hbm, mask_hbm,
    qm, kv, lists, stats,
    feats, gain, w, src, adj, fine, mask, normed, nbr, picked, half, along_z, ag,
    send_n, recv_n, relay_send, a_sem, b_send, b_recv, c_send, c_recv, d_send, d_recv, e_send, e_recv,
    k_send, k_recv, f_send, f_recv, s_sem, mine_out, their, in_sem,
):
    r = lax.axis_index("region")
    s = lax.axis_index("sub")
    z_lo, y = r // 4, lax.rem(r, 4)
    z_hi, x, c = s // 8, lax.rem(s // 2, 4), lax.rem(s, 2)
    z = z_hi * 2 + z_lo
    zi = z_lo * 2 + z_hi
    me = r * 16 + s
    has = [r > 0, r < 7, jnp.where(c == 0, s > 0, s < 15)]
    partner = (r, s + 1 - 2 * c)
    y_next, y_prev = (place(x, lax.rem(y + k, 4), z, c) for k in (1, 3))
    z_next, z_prev, z_far = (place(x, y, lax.rem(z + k, 4), c) for k in (1, 3, 2))
    x_next, x_prev = (place(lax.rem(x + k, 4), y, z, c) for k in (1, 3))
    nbr_dev = [(r - 1, s), (r + 1, s), (r, s - 1 + 2 * c)]

    loads = [
        pltpu.make_async_copy(a, b, in_sem.at[i])
        for i, (a, b) in enumerate(
            ((src_hbm, src), (gain_hbm, gain), (feats_hbm, feats), (w_hbm, w), (adj_hbm, adj), (fine_hbm, fine), (mask_hbm, mask))
        )
    ]
    for load in loads:
        load.start()

    for d in range(3):

        @pl.when(jnp.logical_not(has[d]))
        def _():
            nbr[d] = jnp.zeros((ROWS, D), BF)

    barrier = pltpu.get_barrier_semaphore()
    for dev in (partner, y_next, y_prev, z_next, z_prev, z_far, x_next, x_prev):
        pl.semaphore_signal(barrier, inc=1, device_id=dev, device_id_type=MESH)
    for d in range(3):

        @pl.when(has[d])
        def _():
            pl.semaphore_signal(barrier, inc=1, device_id=nbr_dev[d], device_id_type=MESH)

    for load in loads[:3]:
        load.wait()
    src_row = (src[...] - me * ROWS).astype(F32)
    rows32 = lax.broadcasted_iota(I32, (32, CN), 0)
    cols32 = lax.broadcasted_iota(I32, (32, CN), 1)
    src_col = jnp.sum(jnp.where(rows32 == cols32, src_row, 0.0), axis=1, keepdims=True).astype(I32)
    hot = (lax.broadcasted_iota(I32, (32, ROWS), 1) == src_col).astype(BF)
    mine = rms(jnp.dot(hot, feats[...], preferred_element_type=F32), gain[...])
    picked[0] = mine[:, : D // 2]
    picked[1] = mine[:, D // 2 :]

    n_near = 8 + sum(h.astype(I32) for h in has)
    pl.semaphore_wait(barrier, n_near)

    def copy(src_ref, dst_ref, ss, rs, dev):
        return pltpu.make_async_remote_copy(
            src_ref=src_ref, dst_ref=dst_ref, send_sem=ss, recv_sem=rs, device_id=dev, device_id_type=MESH
        )

    a_copy = copy(picked.at[1 - c], half, a_sem.at[0], a_sem.at[1], partner)
    a_copy.start()

    def land(d):
        return d ^ 1 if d < 2 else 2

    def send_side(d, ch, dev, slot=None):
        slot = land(d) if slot is None else slot
        rows = pl.ds(pl.multiple_of(ch * CHUNK, CHUNK), CHUNK)
        return copy(normed.at[rows], nbr.at[slot, rows], send_n.at[d, ch], recv_n.at[slot, ch], dev)

    def relay_side(d, ch, dev):
        rows = pl.ds(pl.multiple_of(ch * CHUNK, CHUNK), CHUNK)
        return copy(nbr.at[d, rows], nbr.at[d ^ 1, rows], relay_send.at[ch - 2], recv_n.at[d ^ 1, ch], dev)

    def side_to(d, ch):
        if d >= 2:
            return nbr_dev[d], 2
        turn = ((r == 4) if d == 0 else (r == 3)) & (ch >= 2)
        far = 0 if d == 0 else 7
        return (jnp.where(turn, far, nbr_dev[d][0]), s), jnp.where(turn, d, d ^ 1)

    def start_sides(dirs, ch, crossing=None):
        for d in dirs:
            now = has[d]
            if crossing is not None:
                over = (r == 4) if d == 0 else (r == 3) if d == 1 else (r < 0)
                now = now & (over if crossing else jnp.logical_not(over))

            @pl.when(now)
            def _():
                send_side(d, ch, *side_to(d, ch)).start()

    def norm_chunk(ch):
        rows = pl.ds(ch * CHUNK, CHUNK)
        normed[rows] = rms(feats[rows].astype(F32), gain[...])

    norm_chunk(2)
    a_copy.wait()
    r48 = lax.broadcasted_iota(I32, (CPAD, 64), 0)
    c48 = lax.broadcasted_iota(I32, (CPAD, 64), 1)
    first = r48 < CN
    pick = jnp.where(first, r48, r48 + 12) == c48
    pick = (pick & (r48 < 2 * CN)).astype(BF)
    own_half = picked[c]
    lo = jnp.where(c == 0, own_half, half[...])
    hi = jnp.where(c == 0, half[...], own_half)
    block = jnp.dot(pick, jnp.concatenate([lo, hi], axis=0), preferred_element_type=F32).astype(BF)
    along_z[zi] = block

    blk_ref = along_z.at[zi]
    b_copies = [copy(blk_ref, blk_ref, b_send.at[i], b_recv.at[i], dev) for i, dev in enumerate((z_next, z_prev, z_far))]
    for b in b_copies:
        b.start()
    for ch in (3, 0, 1):
        norm_chunk(ch)
    for load in loads[3:]:
        load.wait()

    heads_of = (lax.broadcasted_iota(I32, (D, 128), 0) // HW == lax.broadcasted_iota(I32, (D, 128), 1)).astype(BF)
    stats[...] = jnp.zeros_like(stats)

    def top_norm(vals):
        sq = (vals.astype(F32) * vals.astype(F32)).astype(BF)
        sums = jnp.dot(sq, heads_of, preferred_element_type=F32)
        return jnp.max(sums, axis=0, keepdims=True)

    def put_kv(vals, block, count):
        kv[pl.ds(block, count)] = vals.reshape(count, BLOCK, 2 * D)
        stats[0:1] = jnp.maximum(stats[0:1], top_norm(vals[:, :D]))

    def k_copy(ch):
        there = pl.ds((3 + c) * BLK + 4 * ch, 4)
        return copy(kv.at[pl.ds(4 * ch, 4)], kv.at[there], k_send.at[ch], k_recv.at[ch], partner)

    lane_head = lax.broadcasted_iota(I32, (CHUNK, 256), 1) // HW

    def own_chunk(ch):
        vals = normed[pl.ds(ch * CHUNK, CHUNK)]
        qv = jnp.dot(vals, w[:, :D], preferred_element_type=F32).astype(BF) * jnp.asarray(HW**-0.5, BF)
        stats[1:2] = jnp.maximum(stats[1:2], top_norm(qv))
        for g in range(2):
            for h in range(4):
                qh = jnp.where(lane_head == h, qv[:, g * 256 : (g + 1) * 256], jnp.zeros((), BF))
                qm[pl.ds(4 * ch, 4), g, h * BLOCK : (h + 1) * BLOCK, :] = qh.reshape(4, BLOCK, 256)
        put_kv(jnp.dot(vals, w[:, D:], preferred_element_type=F32).astype(BF), 4 * ch, 4)
        k_copy(ch).start()

    for b in b_copies:
        b.wait()
    r80 = lax.broadcasted_iota(I32, (80, 2 * CPAD), 0)
    c80 = lax.broadcasted_iota(I32, (80, 2 * CPAD), 1)
    tight = ((r80 // 40) * CPAD + lax.rem(r80, 40) == c80).astype(BF)
    for h in range(2):
        both = jnp.concatenate([along_z[2 * h], along_z[2 * h + 1]], axis=0)
        ag[c, x, h, y] = jnp.dot(tight, both, preferred_element_type=F32).astype(BF)

    def side_part(ch, dirs, crossing=None):
        for d in dirs:
            over = (r == 4) if d == 0 else (r == 3) if d == 1 else (r < 0)

            def take():
                @pl.when(has[d])
                def _():
                    send_side(land(d), ch, nbr_dev[d]).wait_recv()

                rows = pl.ds(pl.multiple_of(ch * CHUNK, CHUNK), CHUNK)
                vals = jnp.dot(nbr[d, rows], w[:, D:], preferred_element_type=F32).astype(BF)
                put_kv(vals, ((d + 1) if d < 2 else (3 + c)) * BLK + 4 * ch, 4)

            if crossing is None:
                take()
            else:
                pl.when(over if crossing else jnp.logical_not(over))(take)

    def rings(kinds, early, late):
        sets = []
        for slab, at, nxt, prv, snd, rcv in kinds:
            prev_at, next_at = lax.rem(at + 3, 4), lax.rem(at + 1, 4)
            sets.append((
                [copy(slab(at, h), slab(at, h), snd.at[0, h], rcv.at[0, h], nxt) for h in range(2)],
                [copy(slab(at, h), slab(at, h), snd.at[1, h], rcv.at[1, h], prv) for h in range(2)],
                copy(slab(prev_at, 0), slab(prev_at, 0), snd.at[2, 0], rcv.at[2, 0], nxt),
                copy(slab(next_at, 1), slab(next_at, 1), snd.at[2, 1], rcv.at[2, 1], prv),
            ))
        for to_next, to_prev, _, _ in sets:
            to_next[0].start()
            to_prev[1].start()
        for to_next, to_prev, _, _ in sets:
            to_next[1].start()
            to_prev[0].start()
        early()
        for to_next, to_prev, on_next, on_prev in sets:
            to_next[0].wait_recv()
            on_next.start()
            to_prev[1].wait_recv()
            on_prev.start()
        for to_next, to_prev, _, _ in sets:
            to_next[1].wait_recv()
            to_prev[0].wait_recv()
        late()
        for to_next, to_prev, on_next, on_prev in sets:
            on_next.wait_recv()
            on_prev.wait_recv()
            for a in to_next + to_prev + [on_next, on_prev]:
                a.wait_send()

    def find_lists():
        dev_of, local = adj[...] // BLK, lax.rem(adj[...], BLK)
        gap = dev_of - me
        side = jnp.where(gap == -16, 1, jnp.where(gap == 16, 2, jnp.where(gap == -1, 3, jnp.where(gap == 1, 4, 0))))
        slot = side * BLK + local
        fine_live = (fine[...] == 1) | (lax.broadcasted_iota(I32, (NADJ, BLK), 0) == 0)
        fine_n = fine_live.astype(I32)
        eye = (lax.broadcasted_iota(I32, (BLK, BLK), 0) == lax.broadcasted_iota(I32, (BLK, BLK), 1)).astype(BF)
        coarse_n = lax.dot_general(
            (mask[...] == 1).astype(BF), eye, (((0,), (0,)), ((), ())), preferred_element_type=F32
        ).astype(I32)
        spot = lax.broadcasted_iota(I32, (56, BLK), 0)
        found = jnp.full((56, BLK), NB, I32)
        count = jnp.zeros((1, BLK), I32)
        for j in range(CBLK):
            live = coarse_n[j : j + 1]
            found = jnp.where(spot == jnp.where(live == 1, count, -1), WIN + j, found)
            count = count + live
        for j in range(NADJ):
            live = fine_n[j : j + 1]
            found = jnp.where(spot == jnp.where(live == 1, count, -1), slot[j : j + 1], found)
            count = count + live
        lists[...] = jnp.zeros_like(lists)
        lists[:, :BLK] = jnp.where(spot == 48, count, found)
        kv[NB] = jnp.zeros((BLOCK, 2 * D), BF)

    def c_early():
        for ch in (2, 3):
            start_sides((0, 1), ch, True)
        start_sides((2,), 2)
        own_chunk(0)
        find_lists()

    rings(
        [
            (lambda i, h: ag.at[c, x, h, i], y, y_next, y_prev, c_send.at[0], c_recv.at[0]),
        ],
        c_early, lambda: None,
    )

    def e_copy(i):
        part = ag.at[c, i, 1 - c]
        return copy(part, part, e_send.at[i], e_recv.at[i], partner)

    def e_start(i):
        e_copy(i).start()

    def d_early():
        e_start(x)
        for ch in (0, 1):
            start_sides((0, 1), ch, True)

        def sides(i, carry):
            start_sides((0, 1), lax.rem(i + 2, NCH), False)
            return carry

        lax.fori_loop(0, NCH, sides, 0)
        own_chunk(1)
        own_chunk(2)
        own_chunk(3)

    def pass_on():
        for at, d, to in ((7, 1, 4), (0, 0, 3)):

            @pl.when(r == at)
            def _():
                for ch in (2, 3):
                    send_side(d ^ 1, ch, (to, s)).wait_recv()
                    relay_side(d, ch, (to, s)).start()

    def d_late():
        e_start(lax.rem(x + 3, 4))
        e_start(lax.rem(x + 1, 4))
        for ch in (3, 0, 1):
            start_sides((2,), ch)

    rings(
        [
            (lambda i, h: ag.at[c, i, h], x, x_next, x_prev, d_send.at[0], d_recv.at[0]),
        ],
        d_early, d_late,
    )
    e_start(lax.rem(x + 2, 4))
    pass_on()
    side_part(2, (0, 1), False)

    def e_wait(i, carry):
        e_copy(i).wait()
        return carry

    lax.fori_loop(0, 4, e_wait, 0)

    def f_copy(yy):
        part = kv.at[pl.ds(WIN + 5 * (4 * c + yy), 5)]
        return copy(part, part, f_send.at[yy], f_recv.at[yy], partner)

    def coarse_part(yy, carry):
        cols = []
        for h in range(2):
            got = [ag[h, k, c, yy] for k in range(4)]
            cols.append(jnp.concatenate([g[40 * zh : 40 * zh + 40] for zh in range(2) for g in got], axis=0))
        vals = jnp.concatenate(cols, axis=1)
        put_kv(jnp.dot(vals, w[:, D:], preferred_element_type=F32).astype(BF), WIN + 5 * (4 * c + yy), 5)
        f_copy(yy).start()
        return carry

    lax.fori_loop(0, 4, coarse_part, 0)
    mine_out[...] = stats[...]
    s_copy = copy(mine_out, their, s_sem.at[0], s_sem.at[1], partner)
    s_copy.start()
    side_part(3, (0, 1), False)
    side_part(2, (2,))
    side_part(3, (2,))

    def rest(i, carry):
        side_part(i, (0, 1, 2))
        return carry

    lax.fori_loop(0, 2, rest, 0)

    def crossed(i, carry):
        side_part(i + 2, (0, 1), True)
        return carry

    lax.fori_loop(0, 2, crossed, 0)
    s_copy.wait()
    stats[...] = jnp.maximum(stats[...], their[...])

    def send_wait(ch, carry):
        k_copy(ch).wait()
        f_copy(ch).wait()
        for d in range(3):

            @pl.when(has[d])
            def _():
                send_side(d, ch, nbr_dev[d]).wait_send()

        return carry

    lax.fori_loop(0, NCH, send_wait, 0)
    for at, d, to in ((7, 1, 4), (0, 0, 3)):

        @pl.when(r == at)
        def _():
            for ch in (2, 3):
                relay_side(d, ch, (to, s)).wait_send()


def attend_kernel(unroll, lists_vmem, qm, kv, stats, gain_hbm, w_hbm, out, lists, gain, w, acc, lsum, sems):
    loads = [
        pltpu.make_async_copy(a, b, sems.at[i])
        for i, (a, b) in enumerate(((lists_vmem, lists), (gain_hbm, gain), (w_hbm, w)))
    ]
    for load in loads:
        load.start()
    lane = lax.broadcasted_iota(I32, (BLOCK, 256), 1) // HW
    acc[...] = jnp.zeros_like(acc)
    lsum[...] = jnp.zeros_like(lsum)
    for load in loads:
        load.wait()

    bound = jnp.max(jnp.sqrt(stats[0:1]) * jnp.sqrt(stats[1:2])) * 1.02
    safe = bound < LOG_CAP

    def groups(b):
        return jnp.where(b < BLK, (lists[48, jnp.minimum(b, BLK - 1)] + GRP - 1) // GRP, 0)

    def blocks_of(b, t, lo):
        bb = jnp.minimum(b, BLK - 1)
        return jnp.concatenate([kv[lists[t * GRP + j, bb], :, lo : lo + 256] for j in range(GRP)], axis=0)

    def scores(b, t, g):
        return lax.dot_general(qm[jnp.minimum(b, BLK - 1), g], blocks_of(b, t, g * 256), NT, preferred_element_type=F32)

    key_lane = lax.broadcasted_iota(I32, (1, GRP * BLOCK), 1)

    def open_keys(b, t):
        bb = jnp.minimum(b, BLK - 1)
        return key_lane < (lists[48, bb] - t * GRP) * BLOCK

    def count_up(b, g, p, keys):
        kept = jnp.where(keys, p, 0.0)
        lsum[b, g] += functools.reduce(
            lambda a, e: a + e, [kept[:, i : i + 128] for i in range(0, GRP * BLOCK, 128)]
        )
        return p.astype(BF)

    def mix(b, t, g, p):
        mixed = jnp.dot(p, blocks_of(b, t, D + g * 256), preferred_element_type=F32)
        kept = mixed[:BLOCK]
        for h in range(1, 4):
            kept = jnp.where(lane == h, mixed[h * BLOCK : (h + 1) * BLOCK], kept)
        acc[b, g] += kept

    def add_up(b, t, g, p, keys):
        mix(b, t, g, count_up(b, g, p, keys))

    @pl.when(safe)
    def _():
        total = functools.reduce(lambda a, b: a + b, [groups(b) for b in range(BLK)])

        def step_on(b, t):
            last = t + 1 >= groups(b)
            return jnp.where(last, jnp.minimum(b + 1, BLK), b), jnp.where(last, 0, t + 1)

        def body(i, at):
            spots = [at]
            for _ in range(unroll):
                spots.append(step_on(*spots[-1]))
            steps = [(u, g) for u in range(unroll) for g in range(2)]
            held = scores(*spots[0], 0)
            for k, (u, g) in enumerate(steps):
                later = None
                if k + 1 < len(steps):
                    nu, ng = steps[k + 1]
                    later = scores(*spots[nu], ng)
                add_up(*spots[u], g, jnp.exp(held), open_keys(*spots[u]))
                held = later
            return spots[-1]

        lax.fori_loop(0, (total + unroll - 1) // unroll, body, (jnp.int32(0), jnp.int32(0)))

    @pl.when(jnp.logical_not(safe))
    def _():
        def block(b, carry):
            for g in range(2):
                def peak(t, m):
                    sc = jnp.where(open_keys(b, t), scores(b, t, g), neg_large)
                    return jnp.maximum(m, jnp.max(sc, axis=-1, keepdims=True))

                top = lax.fori_loop(0, groups(b), peak, jnp.full((256, 1), neg_large, F32))

                def weigh(t, carry):
                    keys = open_keys(b, t)
                    sc = jnp.where(keys, scores(b, t, g), neg_large)
                    add_up(b, t, g, jnp.exp(sc - top), keys)
                    return carry

                lax.fori_loop(0, groups(b), weigh, 0)
            return carry

        lax.fori_loop(0, BLK, block, 0)

    def finish(i):
        attended = []
        for b in range(4 * i, 4 * i + 4):
            pieces = []
            for g in range(2):
                total = jnp.sum(lsum[b, g, :BLOCK, :], axis=-1, keepdims=True)
                for h in range(1, 4):
                    rows = slice(h * BLOCK, (h + 1) * BLOCK)
                    total = jnp.where(lane == h, jnp.sum(lsum[b, g, rows, :], axis=-1, keepdims=True), total)
                pieces.append(acc[b, g] / total)
            row = jnp.concatenate(pieces, axis=1).astype(BF).astype(F32)
            attended.append(rms(row, gain[...]))
        rows = slice(i * CHUNK, (i + 1) * CHUNK)
        out[rows] = jnp.dot(jnp.concatenate(attended, axis=0), w[...], preferred_element_type=F32).astype(BF)

    for i in range(4):
        finish(i)


def attend_call(lists, qm, kv, stats, gain_out, w_out):
    vmem = pl.BlockSpec(memory_space=pltpu.VMEM)
    hbm = pl.BlockSpec(memory_space=pltpu.HBM)
    dma = pltpu.SemaphoreType.DMA
    return pl.pallas_call(
        functools.partial(attend_kernel, UNROLL),
        out_shape=jax.ShapeDtypeStruct((ROWS, D), BF),
        in_specs=[vmem, vmem, vmem, vmem, hbm, hbm],
        out_specs=vmem,
        scratch_shapes=[
            pltpu.SMEM((56, 128), I32),
            pltpu.VMEM((1, D), F32),
            pltpu.VMEM((D, D), BF),
            pltpu.VMEM((BLK + 1, 2, BLOCK, 256), F32),
            pltpu.VMEM((BLK + 1, 2, 256, 128), F32),
            dma((3,)),
        ],
        compiler_params=pltpu.CompilerParams(vmem_limit_bytes=28 * 2**20),
    )(lists, qm, kv, stats, gain_out, w_out)


def per_device(node_feats, gain_in, w_qkv, gain_out, w_out, adjacency, fine_valid, coarse_mask, coarse_src):
    vmem = pl.BlockSpec(memory_space=pltpu.VMEM)
    hbm = pl.BlockSpec(memory_space=pltpu.HBM)
    dma = pltpu.SemaphoreType.DMA
    qm, kv, lists, stats = pl.pallas_call(
        gather_kernel,
        out_shape=(
            jax.ShapeDtypeStruct((BLK, 2, 256, 256), BF),
            jax.ShapeDtypeStruct((NB + 1, BLOCK, 2 * D), BF),
            jax.ShapeDtypeStruct((56, 128), I32),
            jax.ShapeDtypeStruct((8, 128), F32),
        ),
        in_specs=[hbm] * 7,
        out_specs=(vmem,) * 4,
        scratch_shapes=[
            pltpu.VMEM((ROWS, D), BF),
            pltpu.VMEM((1, D), F32),
            pltpu.VMEM((D, 3 * D), BF),
            pltpu.VMEM((1, CN), I32),
            pltpu.VMEM((NADJ, BLK), I32),
            pltpu.VMEM((NADJ, BLK), I32),
            pltpu.VMEM((BLK, CBLK), I32),
            pltpu.VMEM((ROWS, D), BF),
            pltpu.VMEM((3, ROWS, D), BF),
            pltpu.VMEM((2, 32, D // 2), BF),
            pltpu.VMEM((32, D // 2), BF),
            pltpu.VMEM((4, CPAD, D // 2), BF),
            pltpu.VMEM((2, 4, 2, 4, 80, D // 2), BF),
            dma((3, 4)), dma((3, 4)), dma((2,)), dma((2,)), dma((3,)), dma((3,)),
            dma((1, 3, 2)), dma((1, 3, 2)), dma((1, 3, 2)), dma((1, 3, 2)), dma((4,)), dma((4,)),
            dma((4,)), dma((4,)), dma((4,)), dma((4,)), dma((2,)),
            pltpu.VMEM((8, 128), F32), pltpu.VMEM((8, 128), F32),
            dma((7,)),
        ],
        compiler_params=pltpu.CompilerParams(
            collective_id=0, has_side_effects=True, vmem_limit_bytes=24 * 2**20
        ),
    )(
        *(
            pltpu.with_memory_space_constraint(a, pltpu.HBM)
            for a in (
                node_feats, gain_in.reshape(1, D), w_qkv, coarse_src.reshape(1, CN),
                adjacency.T, fine_valid.T, coarse_mask,
            )
        )
    )
    return attend_call(
        lists, qm, kv, stats,
        *(pltpu.with_memory_space_constraint(a, pltpu.HBM) for a in (gain_out.reshape(1, D), w_out)),
    )


def solution(mesh):
    both = ("region", "sub")
    in_specs = (P(both, None), P(), P(), P(), P(), P(both, None), P(both, None), P(both, None), P(both))
    return jax.shard_map(per_device, mesh=mesh, in_specs=in_specs, out_specs=P(both, None), check_vma=False)
```

```python
import functools

import jax
import jax.numpy as jnp
from jax import lax
from jax.experimental import pallas as pl
from jax.experimental.pallas import tpu as pltpu
from jax.sharding import PartitionSpec as P

D = 512
HEADS = 8
HW = D // HEADS
BLOCK = 64
NADJ = 7
BLK = 16
ROWS = BLK * BLOCK
CN = 20
CBLK = 40
WIN = 5 * BLK
NB = WIN + CBLK
CHUNK = 256
NCH = ROWS // CHUNK
CPAD = 48
GRP = 4
UNROLL = 16
LOG_CAP = 60.0
BF = jnp.bfloat16
F32 = jnp.float32
I32 = jnp.int32
MESH = pl.DeviceIdType.MESH
NT = (((1,), (1,)), ((), ()))
neg_large = -1e30


def rms(vals, gain):
    mean_square = jnp.mean(vals * vals, axis=-1, keepdims=True)
    return (vals * lax.rsqrt(mean_square + 1e-06) * gain).astype(BF)


def place(x, y, z, c):
    return (lax.rem(z, 2) * 4 + y, (z // 2) * 8 + x * 2 + c)


def gather_kernel(
    feats_hbm, gain_hbm, w_hbm, src_hbm, adj_hbm, fine_hbm, mask_hbm,
    qm, kv, lists, stats,
    feats, gain, w, src, adj, fine, mask, normed, nbr, picked, half, along_z, ag,
    send_n, recv_n, relay_send, a_sem, b_send, b_recv, c_send, c_recv, d_send, d_recv, e_send, e_recv,
    k_send, k_recv, f_send, f_recv, s_sem, mine_out, their, in_sem,
):
    r = lax.axis_index("region")
    s = lax.axis_index("sub")
    z_lo, y = r // 4, lax.rem(r, 4)
    z_hi, x, c = s // 8, lax.rem(s // 2, 4), lax.rem(s, 2)
    z = z_hi * 2 + z_lo
    zi = z_lo * 2 + z_hi
    me = r * 16 + s
    has = [r > 0, r < 7, jnp.where(c == 0, s > 0, s < 15)]
    partner = (r, s + 1 - 2 * c)
    y_next, y_prev = (place(x, lax.rem(y + k, 4), z, c) for k in (1, 3))
    z_next, z_prev, z_far = (place(x, y, lax.rem(z + k, 4), c) for k in (1, 3, 2))
    x_next, x_prev = (place(lax.rem(x + k, 4), y, z, c) for k in (1, 3))
    nbr_dev = [(r - 1, s), (r + 1, s), (r, s - 1 + 2 * c)]

    loads = [
        pltpu.make_async_copy(a, b, in_sem.at[i])
        for i, (a, b) in enumerate(
            ((src_hbm, src), (gain_hbm, gain), (feats_hbm, feats), (w_hbm, w), (adj_hbm, adj), (fine_hbm, fine), (mask_hbm, mask))
        )
    ]
    for load in loads:
        load.start()

    for d in range(3):

        @pl.when(jnp.logical_not(has[d]))
        def _():
            nbr[d] = jnp.zeros((ROWS, D), BF)

    barrier = pltpu.get_barrier_semaphore()
    for dev in (partner, y_next, y_prev, z_next, z_prev, z_far, x_next, x_prev):
        pl.semaphore_signal(barrier, inc=1, device_id=dev, device_id_type=MESH)
    for d in range(3):

        @pl.when(has[d])
        def _():
            pl.semaphore_signal(barrier, inc=1, device_id=nbr_dev[d], device_id_type=MESH)

    for load in loads[:3]:
        load.wait()
    src_row = (src[...] - me * ROWS).astype(F32)
    rows32 = lax.broadcasted_iota(I32, (32, CN), 0)
    cols32 = lax.broadcasted_iota(I32, (32, CN), 1)
    src_col = jnp.sum(jnp.where(rows32 == cols32, src_row, 0.0), axis=1, keepdims=True).astype(I32)
    hot = (lax.broadcasted_iota(I32, (32, ROWS), 1) == src_col).astype(BF)
    mine = rms(jnp.dot(hot, feats[...], preferred_element_type=F32), gain[...])
    picked[0] = mine[:, : D // 2]
    picked[1] = mine[:, D // 2 :]

    n_near = 8 + sum(h.astype(I32) for h in has)
    pl.semaphore_wait(barrier, n_near)

    def copy(src_ref, dst_ref, ss, rs, dev):
        return pltpu.make_async_remote_copy(
            src_ref=src_ref, dst_ref=dst_ref, send_sem=ss, recv_sem=rs, device_id=dev, device_id_type=MESH
        )

    a_copy = copy(picked.at[1 - c], half, a_sem.at[0], a_sem.at[1], partner)
    a_copy.start()

    def land(d):
        return d ^ 1 if d < 2 else 2

    def send_side(d, ch, dev, slot=None):
        slot = land(d) if slot is None else slot
        rows = pl.ds(pl.multiple_of(ch * CHUNK, CHUNK), CHUNK)
        return copy(normed.at[rows], nbr.at[slot, rows], send_n.at[d, ch], recv_n.at[slot, ch], dev)

    def relay_side(d, ch, dev):
        rows = pl.ds(pl.multiple_of(ch * CHUNK, CHUNK), CHUNK)
        return copy(nbr.at[d, rows], nbr.at[d ^ 1, rows], relay_send.at[ch - 2], recv_n.at[d ^ 1, ch], dev)

    def side_to(d, ch):
        if d >= 2:
            return nbr_dev[d], 2
        turn = ((r == 4) if d == 0 else (r == 3)) & (ch >= 2)
        far = 0 if d == 0 else 7
        return (jnp.where(turn, far, nbr_dev[d][0]), s), jnp.where(turn, d, d ^ 1)

    def start_sides(dirs, ch, crossing=None):
        for d in dirs:
            now = has[d]
            if crossing is not None:
                over = (r == 4) if d == 0 else (r == 3) if d == 1 else (r < 0)
                now = now & (over if crossing else jnp.logical_not(over))

            @pl.when(now)
            def _():
                send_side(d, ch, *side_to(d, ch)).start()

    def norm_chunk(ch):
        rows = pl.ds(ch * CHUNK, CHUNK)
        normed[rows] = rms(feats[rows].astype(F32), gain[...])

    norm_chunk(2)
    a_copy.wait()
    r48 = lax.broadcasted_iota(I32, (CPAD, 64), 0)
    c48 = lax.broadcasted_iota(I32, (CPAD, 64), 1)
    first = r48 < CN
    pick = jnp.where(first, r48, r48 + 12) == c48
    pick = (pick & (r48 < 2 * CN)).astype(BF)
    own_half = picked[c]
    lo = jnp.where(c == 0, own_half, half[...])
    hi = jnp.where(c == 0, half[...], own_half)
    block = jnp.dot(pick, jnp.concatenate([lo, hi], axis=0), preferred_element_type=F32).astype(BF)
    along_z[zi] = block

    blk_ref = along_z.at[zi]
    b_copies = [copy(blk_ref, blk_ref, b_send.at[i], b_recv.at[i], dev) for i, dev in enumerate((z_next, z_prev, z_far))]
    for b in b_copies:
        b.start()
    for ch in (3, 0, 1):
        norm_chunk(ch)
    for load in loads[3:]:
        load.wait()

    heads_of = (lax.broadcasted_iota(I32, (D, 128), 0) // HW == lax.broadcasted_iota(I32, (D, 128), 1)).astype(BF)
    stats[...] = jnp.zeros_like(stats)

    def top_norm(vals):
        sq = (vals.astype(F32) * vals.astype(F32)).astype(BF)
        sums = jnp.dot(sq, heads_of, preferred_element_type=F32)
        return jnp.max(sums, axis=0, keepdims=True)

    def put_kv(vals, block, count):
        kv[pl.ds(block, count)] = vals.reshape(count, BLOCK, 2 * D)
        stats[0:1] = jnp.maximum(stats[0:1], top_norm(vals[:, :D]))

    def k_copy(ch):
        there = pl.ds((3 + c) * BLK + 4 * ch, 4)
        return copy(kv.at[pl.ds(4 * ch, 4)], kv.at[there], k_send.at[ch], k_recv.at[ch], partner)

    lane_head = lax.broadcasted_iota(I32, (CHUNK, 256), 1) // HW

    def own_chunk(ch):
        vals = normed[pl.ds(ch * CHUNK, CHUNK)]
        qv = jnp.dot(vals, w[:, :D], preferred_element_type=F32).astype(BF) * jnp.asarray(HW**-0.5, BF)
        stats[1:2] = jnp.maximum(stats[1:2], top_norm(qv))
        for g in range(2):
            for h in range(4):
                qh = jnp.where(lane_head == h, qv[:, g * 256 : (g + 1) * 256], jnp.zeros((), BF))
                qm[pl.ds(4 * ch, 4), g, h * BLOCK : (h + 1) * BLOCK, :] = qh.reshape(4, BLOCK, 256)
        put_kv(jnp.dot(vals, w[:, D:], preferred_element_type=F32).astype(BF), 4 * ch, 4)
        k_copy(ch).start()

    for b in b_copies:
        b.wait()
    r80 = lax.broadcasted_iota(I32, (80, 2 * CPAD), 0)
    c80 = lax.broadcasted_iota(I32, (80, 2 * CPAD), 1)
    tight = ((r80 // 40) * CPAD + lax.rem(r80, 40) == c80).astype(BF)
    for h in range(2):
        both = jnp.concatenate([along_z[2 * h], along_z[2 * h + 1]], axis=0)
        ag[c, x, h, y] = jnp.dot(tight, both, preferred_element_type=F32).astype(BF)

    def side_part(ch, dirs, crossing=None):
        for d in dirs:
            over = (r == 4) if d == 0 else (r == 3) if d == 1 else (r < 0)

            def take():
                @pl.when(has[d])
                def _():
                    send_side(land(d), ch, nbr_dev[d]).wait_recv()

                rows = pl.ds(pl.multiple_of(ch * CHUNK, CHUNK), CHUNK)
                vals = jnp.dot(nbr[d, rows], w[:, D:], preferred_element_type=F32).astype(BF)
                put_kv(vals, ((d + 1) if d < 2 else (3 + c)) * BLK + 4 * ch, 4)

            if crossing is None:
                take()
            else:
                pl.when(over if crossing else jnp.logical_not(over))(take)

    def rings(kinds, early, late):
        sets = []
        for slab, at, nxt, prv, snd, rcv in kinds:
            prev_at, next_at = lax.rem(at + 3, 4), lax.rem(at + 1, 4)
            sets.append((
                [copy(slab(at, h), slab(at, h), snd.at[0, h], rcv.at[0, h], nxt) for h in range(2)],
                [copy(slab(at, h), slab(at, h), snd.at[1, h], rcv.at[1, h], prv) for h in range(2)],
                copy(slab(prev_at, 0), slab(prev_at, 0), snd.at[2, 0], rcv.at[2, 0], nxt),
                copy(slab(next_at, 1), slab(next_at, 1), snd.at[2, 1], rcv.at[2, 1], prv),
            ))
        for to_next, to_prev, _, _ in sets:
            to_next[0].start()
            to_prev[1].start()
        for to_next, to_prev, _, _ in sets:
            to_next[1].start()
            to_prev[0].start()
        early()
        for to_next, to_prev, on_next, on_prev in sets:
            to_next[0].wait_recv()
            on_next.start()
            to_prev[1].wait_recv()
            on_prev.start()
        for to_next, to_prev, _, _ in sets:
            to_next[1].wait_recv()
            to_prev[0].wait_recv()
        late()
        for to_next, to_prev, on_next, on_prev in sets:
            on_next.wait_recv()
            on_prev.wait_recv()
            for a in to_next + to_prev + [on_next, on_prev]:
                a.wait_send()

    def find_lists():
        dev_of, local = adj[...] // BLK, lax.rem(adj[...], BLK)
        gap = dev_of - me
        side = jnp.where(gap == -16, 1, jnp.where(gap == 16, 2, jnp.where(gap == -1, 3, jnp.where(gap == 1, 4, 0))))
        slot = side * BLK + local
        fine_live = (fine[...] == 1) | (lax.broadcasted_iota(I32, (NADJ, BLK), 0) == 0)
        fine_n = fine_live.astype(I32)
        eye = (lax.broadcasted_iota(I32, (BLK, BLK), 0) == lax.broadcasted_iota(I32, (BLK, BLK), 1)).astype(BF)
        coarse_n = lax.dot_general(
            (mask[...] == 1).astype(BF), eye, (((0,), (0,)), ((), ())), preferred_element_type=F32
        ).astype(I32)
        spot = lax.broadcasted_iota(I32, (56, BLK), 0)
        found = jnp.full((56, BLK), NB, I32)
        count = jnp.zeros((1, BLK), I32)
        for j in range(CBLK):
            live = coarse_n[j : j + 1]
            found = jnp.where(spot == jnp.where(live == 1, count, -1), WIN + j, found)
            count = count + live
        for j in range(NADJ):
            live = fine_n[j : j + 1]
            found = jnp.where(spot == jnp.where(live == 1, count, -1), slot[j : j + 1], found)
            count = count + live
        lists[...] = jnp.zeros_like(lists)
        lists[:, :BLK] = jnp.where(spot == 48, count, found)
        kv[NB] = jnp.zeros((BLOCK, 2 * D), BF)

    def c_early():
        for ch in (2, 3):
            start_sides((0, 1), ch, True)
        start_sides((2,), 2)
        own_chunk(0)
        find_lists()

    rings(
        [
            (lambda i, h: ag.at[c, x, h, i], y, y_next, y_prev, c_send.at[0], c_recv.at[0]),
        ],
        c_early, lambda: None,
    )

    def e_copy(i):
        part = ag.at[c, i, 1 - c]
        return copy(part, part, e_send.at[i], e_recv.at[i], partner)

    def e_start(i):
        e_copy(i).start()

    def d_early():
        e_start(x)
        for ch in (0, 1):
            start_sides((0, 1), ch, True)

        def sides(i, carry):
            start_sides((0, 1), lax.rem(i + 2, NCH), False)
            return carry

        lax.fori_loop(0, NCH, sides, 0)
        own_chunk(1)
        own_chunk(2)
        own_chunk(3)

    def pass_on():
        for at, d, to in ((7, 1, 4), (0, 0, 3)):

            @pl.when(r == at)
            def _():
                for ch in (2, 3):
                    send_side(d ^ 1, ch, (to, s)).wait_recv()
                    relay_side(d, ch, (to, s)).start()

    def d_late():
        e_start(lax.rem(x + 3, 4))
        e_start(lax.rem(x + 1, 4))
        for ch in (3, 0, 1):
            start_sides((2,), ch)

    rings(
        [
            (lambda i, h: ag.at[c, i, h], x, x_next, x_prev, d_send.at[0], d_recv.at[0]),
        ],
        d_early, d_late,
    )
    e_start(lax.rem(x + 2, 4))
    pass_on()
    side_part(2, (0, 1), False)

    def e_wait(i, carry):
        e_copy(i).wait()
        return carry

    lax.fori_loop(0, 4, e_wait, 0)

    def f_copy(yy):
        part = kv.at[pl.ds(WIN + 5 * (4 * c + yy), 5)]
        return copy(part, part, f_send.at[yy], f_recv.at[yy], partner)

    def coarse_part(yy, carry):
        cols = []
        for h in range(2):
            got = [ag[h, k, c, yy] for k in range(4)]
            cols.append(jnp.concatenate([g[40 * zh : 40 * zh + 40] for zh in range(2) for g in got], axis=0))
        vals = jnp.concatenate(cols, axis=1)
        put_kv(jnp.dot(vals, w[:, D:], preferred_element_type=F32).astype(BF), WIN + 5 * (4 * c + yy), 5)
        f_copy(yy).start()
        return carry

    lax.fori_loop(0, 4, coarse_part, 0)
    mine_out[...] = stats[...]
    s_copy = copy(mine_out, their, s_sem.at[0], s_sem.at[1], partner)
    s_copy.start()
    side_part(3, (0, 1), False)
    side_part(2, (2,))
    side_part(3, (2,))

    def rest(i, carry):
        side_part(i, (0, 1, 2))
        return carry

    lax.fori_loop(0, 2, rest, 0)

    def crossed(i, carry):
        side_part(i + 2, (0, 1), True)
        return carry

    lax.fori_loop(0, 2, crossed, 0)
    s_copy.wait()
    stats[...] = jnp.maximum(stats[...], their[...])

    def send_wait(ch, carry):
        k_copy(ch).wait()
        f_copy(ch).wait()
        for d in range(3):

            @pl.when(has[d])
            def _():
                send_side(d, ch, nbr_dev[d]).wait_send()

        return carry

    lax.fori_loop(0, NCH, send_wait, 0)
    for at, d, to in ((7, 1, 4), (0, 0, 3)):

        @pl.when(r == at)
        def _():
            for ch in (2, 3):
                relay_side(d, ch, (to, s)).wait_send()


def attend_kernel(unroll, lists_vmem, qm, kv, stats, gain_hbm, w_hbm, out, lists, gain, w, acc, lsum, sems):
    loads = [
        pltpu.make_async_copy(a, b, sems.at[i])
        for i, (a, b) in enumerate(((lists_vmem, lists), (gain_hbm, gain), (w_hbm, w)))
    ]
    for load in loads:
        load.start()
    lane = lax.broadcasted_iota(I32, (BLOCK, 256), 1) // HW
    acc[...] = jnp.zeros_like(acc)
    lsum[...] = jnp.zeros_like(lsum)
    for load in loads:
        load.wait()

    bound = jnp.max(jnp.sqrt(stats[0:1]) * jnp.sqrt(stats[1:2])) * 1.02
    safe = bound < LOG_CAP

    def groups(b):
        return jnp.where(b < BLK, (lists[48, jnp.minimum(b, BLK - 1)] + GRP - 1) // GRP, 0)

    def blocks_of(b, t, lo):
        bb = jnp.minimum(b, BLK - 1)
        return jnp.concatenate([kv[lists[t * GRP + j, bb], :, lo : lo + 256] for j in range(GRP)], axis=0)

    def scores(b, t, g):
        return lax.dot_general(qm[jnp.minimum(b, BLK - 1), g], blocks_of(b, t, g * 256), NT, preferred_element_type=F32)

    key_lane = lax.broadcasted_iota(I32, (1, GRP * BLOCK), 1)

    def open_keys(b, t):
        bb = jnp.minimum(b, BLK - 1)
        return key_lane < (lists[48, bb] - t * GRP) * BLOCK

    def count_up(b, g, p, keys):
        kept = jnp.where(keys, p, 0.0)
        lsum[b, g] += functools.reduce(
            lambda a, e: a + e, [kept[:, i : i + 128] for i in range(0, GRP * BLOCK, 128)]
        )
        return p.astype(BF)

    def mix(b, t, g, p):
        mixed = jnp.dot(p, blocks_of(b, t, D + g * 256), preferred_element_type=F32)
        kept = mixed[:BLOCK]
        for h in range(1, 4):
            kept = jnp.where(lane == h, mixed[h * BLOCK : (h + 1) * BLOCK], kept)
        acc[b, g] += kept

    def add_up(b, t, g, p, keys):
        mix(b, t, g, count_up(b, g, p, keys))

    @pl.when(safe)
    def _():
        total = functools.reduce(lambda a, b: a + b, [groups(b) for b in range(BLK)])

        def step_on(b, t):
            last = t + 1 >= groups(b)
            return jnp.where(last, jnp.minimum(b + 1, BLK), b), jnp.where(last, 0, t + 1)

        def body(i, at):
            spots = [at]
            for _ in range(unroll):
                spots.append(step_on(*spots[-1]))
            steps = [(u, g) for u in range(unroll) for g in range(2)]
            held = scores(*spots[0], 0)
            for k, (u, g) in enumerate(steps):
                later = None
                if k + 1 < len(steps):
                    nu, ng = steps[k + 1]
                    later = scores(*spots[nu], ng)
                add_up(*spots[u], g, jnp.exp(held), open_keys(*spots[u]))
                held = later
            return spots[-1]

        lax.fori_loop(0, (total + unroll - 1) // unroll, body, (jnp.int32(0), jnp.int32(0)))

    @pl.when(jnp.logical_not(safe))
    def _():
        def block(b, carry):
            for g in range(2):
                def peak(t, m):
                    sc = jnp.where(open_keys(b, t), scores(b, t, g), neg_large)
                    return jnp.maximum(m, jnp.max(sc, axis=-1, keepdims=True))

                top = lax.fori_loop(0, groups(b), peak, jnp.full((256, 1), neg_large, F32))

                def weigh(t, carry):
                    keys = open_keys(b, t)
                    sc = jnp.where(keys, scores(b, t, g), neg_large)
                    add_up(b, t, g, jnp.exp(sc - top), keys)
                    return carry

                lax.fori_loop(0, groups(b), weigh, 0)
            return carry

        lax.fori_loop(0, BLK, block, 0)

    def finish(i):
        attended = []
        for b in range(4 * i, 4 * i + 4):
            pieces = []
            for g in range(2):
                total = jnp.sum(lsum[b, g, :BLOCK, :], axis=-1, keepdims=True)
                for h in range(1, 4):
                    rows = slice(h * BLOCK, (h + 1) * BLOCK)
                    total = jnp.where(lane == h, jnp.sum(lsum[b, g, rows, :], axis=-1, keepdims=True), total)
                pieces.append(acc[b, g] / total)
            row = jnp.concatenate(pieces, axis=1).astype(BF).astype(F32)
            attended.append(rms(row, gain[...]))
        rows = slice(i * CHUNK, (i + 1) * CHUNK)
        out[rows] = jnp.dot(jnp.concatenate(attended, axis=0), w[...], preferred_element_type=F32).astype(BF)

    for i in range(4):
        finish(i)


def attend_call(lists, qm, kv, stats, gain_out, w_out):
    vmem = pl.BlockSpec(memory_space=pltpu.VMEM)
    hbm = pl.BlockSpec(memory_space=pltpu.HBM)
    dma = pltpu.SemaphoreType.DMA
    return pl.pallas_call(
        functools.partial(attend_kernel, UNROLL),
        out_shape=jax.ShapeDtypeStruct((ROWS, D), BF),
        in_specs=[vmem, vmem, vmem, vmem, hbm, hbm],
        out_specs=vmem,
        scratch_shapes=[
            pltpu.SMEM((56, 128), I32),
            pltpu.VMEM((1, D), F32),
            pltpu.VMEM((D, D), BF),
            pltpu.VMEM((BLK + 1, 2, BLOCK, 256), F32),
            pltpu.VMEM((BLK + 1, 2, 256, 128), F32),
            dma((3,)),
        ],
        compiler_params=pltpu.CompilerParams(vmem_limit_bytes=28 * 2**20),
    )(lists, qm, kv, stats, gain_out, w_out)


def per_device(node_feats, gain_in, w_qkv, gain_out, w_out, adjacency, fine_valid, coarse_mask, coarse_src):
    vmem = pl.BlockSpec(memory_space=pltpu.VMEM)
    hbm = pl.BlockSpec(memory_space=pltpu.HBM)
    dma = pltpu.SemaphoreType.DMA
    qm, kv, lists, stats = pl.pallas_call(
        gather_kernel,
        out_shape=(
            jax.ShapeDtypeStruct((BLK, 2, 256, 256), BF),
            jax.ShapeDtypeStruct((NB + 1, BLOCK, 2 * D), BF),
            jax.ShapeDtypeStruct((56, 128), I32),
            jax.ShapeDtypeStruct((8, 128), F32),
        ),
        in_specs=[hbm] * 7,
        out_specs=(vmem,) * 4,
        scratch_shapes=[
            pltpu.VMEM((ROWS, D), BF),
            pltpu.VMEM((1, D), F32),
            pltpu.VMEM((D, 3 * D), BF),
            pltpu.VMEM((1, CN), I32),
            pltpu.VMEM((NADJ, BLK), I32),
            pltpu.VMEM((NADJ, BLK), I32),
            pltpu.VMEM((BLK, CBLK), I32),
            pltpu.VMEM((ROWS, D), BF),
            pltpu.VMEM((3, ROWS, D), BF),
            pltpu.VMEM((2, 32, D // 2), BF),
            pltpu.VMEM((32, D // 2), BF),
            pltpu.VMEM((4, CPAD, D // 2), BF),
            pltpu.VMEM((2, 4, 2, 4, 80, D // 2), BF),
            dma((3, 4)), dma((3, 4)), dma((2,)), dma((2,)), dma((3,)), dma((3,)),
            dma((1, 3, 2)), dma((1, 3, 2)), dma((1, 3, 2)), dma((1, 3, 2)), dma((4,)), dma((4,)),
            dma((4,)), dma((4,)), dma((4,)), dma((4,)), dma((2,)),
            pltpu.VMEM((8, 128), F32), pltpu.VMEM((8, 128), F32),
            dma((7,)),
        ],
        compiler_params=pltpu.CompilerParams(
            collective_id=0, has_side_effects=True, vmem_limit_bytes=24 * 2**20
        ),
    )(
        *(
            pltpu.with_memory_space_constraint(a, pltpu.HBM)
            for a in (
                node_feats, gain_in.reshape(1, D), w_qkv, coarse_src.reshape(1, CN),
                adjacency.T, fine_valid.T, coarse_mask,
            )
        )
    )
    return attend_call(
        lists, qm, kv, stats,
        *(pltpu.with_memory_space_constraint(a, pltpu.HBM) for a in (gain_out.reshape(1, D), w_out)),
    )


def solution(mesh):
    both = ("region", "sub")
    in_specs = (P(both, None), P(), P(), P(), P(), P(both, None), P(both, None), P(both, None), P(both))
    return jax.shard_map(per_device, mesh=mesh, in_specs=in_specs, out_specs=P(both, None), check_vma=False)
```
